512 devices in a mesh: acq: 32 (over z, x_lo, core), col: 16 (over x_hi, y).
Axes of the slice: x: 4 (x_hi: 2, x_lo: 2; x = x_hi * 2 + x_lo), y: 8, z: 8, core: 2. Of those that a mesh axis runs over, the one named last changes fastest.
Arguments:
- samples: float32 [128, 2, 24, 2048], P('acq', None, None, 'col'), may hold values from -3 to 3, as said below
- pair_live: int32 [128, 12], replicated, may hold values from 0 to 1, as said below
Outputs:
- displacement: float32 [128, 2, 24, 2048], P('acq', None, None, 'col')
- residual: float32 [128, 12, 2, 24, 2048], P('acq', None, None, None, 'col')
The draws below stay inside these ranges and needn't reach their ends.
Inputs may be any that keep to these rules, and one draw needn't show every extreme that they name: pair_live[e, k] is 0 wherever e + k + 1 >= 128, and 1 for k = 0 wherever e + 1 < 128. `samples`: every sample's magnitude lies between 0.3 and 3.
All inputs are finite; a program needn't handle non-finite values.
Results may differ from the reference program's by a relative error of at most 0.0003.
Values sent between devices are 32-bit elements; how exact they have to be, the bound alone decides.
A program may use at most 64 MiB of HBM per device.

```python
import math
import jax
import jax.numpy as jnp
from jax import lax

ROWS = 24
LAGS = 12
LOOK_ROWS = 5
LOOK_COLS = 20
ACQS = 128
COLS = 2048


def draw_pair_live(key, part):
    long_key = jax.random.fold_in(key, 11)
    other_key = jax.random.fold_in(key, 12)
    long_coins = jax.random.randint(long_key, (ACQS, LAGS), 0, 5)
    other_coins = jax.random.randint(other_key, (ACQS, LAGS), 0, 32)
    lag_pos = lax.broadcasted_iota(jnp.int32, (ACQS, LAGS), 1)
    acq_pos = lax.broadcasted_iota(jnp.int32, (ACQS, LAGS), 0)
    inside = acq_pos + lag_pos + 1 < ACQS
    longest = (lag_pos == LAGS - 1) & (long_coins > 0)
    chosen = (lag_pos == 0) | longest | (other_coins == 0)
    return (inside & chosen).astype(jnp.int32)


def draw_samples(key, part):
    mag_key = jax.random.fold_in(key, 21)
    phase_key = jax.random.fold_in(key, 22)
    shape_all = (ACQS, ROWS, COLS)
    log_mag = jax.random.uniform(mag_key, shape_all, jnp.float32, math.log(0.3), math.log(3.0))
    magnitude = jnp.clip(jnp.exp(log_mag), 0.3, 3.0)
    phase = 0.8 * jax.random.normal(phase_key, shape_all, jnp.float32)
    return jnp.stack([magnitude * jnp.cos(phase), magnitude * jnp.sin(phase)], axis=1)


def setup_inputs(seed: int = 0) -> dict:
    key_of = jax.random.split(jax.random.key(seed), 3)
    return {
        "samples": draw_samples(jax.random.fold_in(key_of[2], 71), 0),
        "pair_live": draw_pair_live(jax.random.fold_in(key_of[2], 71), 0),
    }


def look_sum(source):
    half_rows = (LOOK_ROWS - 1) // 2
    half_cols = LOOK_COLS // 2
    pad_spec = ((0, 0),) * (source.ndim - 2) + ((half_rows, half_rows), (half_cols, half_cols))
    padded = jnp.pad(source, pad_spec)
    count_rows = source.shape[-2]
    count_cols = source.shape[-1]
    by_rows = padded[..., 0:count_rows, :]
    for offset in range(1, LOOK_ROWS):
        by_rows = by_rows + padded[..., offset:offset + count_rows, :]
    total = by_rows[..., 0:count_cols]
    for offset in range(1, LOOK_COLS):
        total = total + by_rows[..., offset:offset + count_cols]
    return total

def design_matrix(live):
    acq_total = live.shape[0]
    lags = live.shape[1]
    acq_pos = lax.broadcasted_iota(jnp.int32, (acq_total, lags, acq_total - 1), 0)
    lag_pos = lax.broadcasted_iota(jnp.int32, (acq_total, lags, acq_total - 1), 1)
    col_pos = lax.broadcasted_iota(jnp.int32, (acq_total, lags, acq_total - 1), 2)
    later_hit = (col_pos == acq_pos + lag_pos).astype(jnp.float32)
    first_hit = (col_pos == acq_pos - 1).astype(jnp.float32)
    live_float = (live > 0).astype(jnp.float32)
    return ((later_hit - first_hit) * live_float[:, :, None]).reshape(acq_total * lags, acq_total - 1)

def reference(samples, pair_live):
    real_part = samples[:, 0]
    imag_part = samples[:, 1]
    power = real_part * real_part + imag_part * imag_part
    power_look = look_sum(power)
    zero_tail = jnp.zeros((LAGS,) + real_part.shape[1:], jnp.float32)
    real_long = jnp.concatenate([real_part, zero_tail], axis=0)
    imag_long = jnp.concatenate([imag_part, zero_tail], axis=0)
    look_long = jnp.concatenate([power_look, zero_tail], axis=0)
    collected = []
    for lag_index in range(LAGS):
        real_later = real_long[lag_index + 1:lag_index + 1 + ACQS]
        imag_later = imag_long[lag_index + 1:lag_index + 1 + ACQS]
        look_later = look_long[lag_index + 1:lag_index + 1 + ACQS]
        cross_real = real_part * real_later + imag_part * imag_later
        cross_imag = imag_part * real_later - real_part * imag_later
        live_mask = (pair_live[:, lag_index] > 0)[:, None, None]
        denominator = jnp.sqrt(jnp.where(live_mask, power_look * look_later, 1.0))
        obs_real = jnp.where(live_mask, look_sum(cross_real) / denominator, 0.0)
        obs_imag = jnp.where(live_mask, look_sum(cross_imag) / denominator, 0.0)
        collected.append(jnp.stack([obs_real, obs_imag], axis=1))
    observed = jnp.stack(collected, axis=1)
    flat_obs = observed.reshape(ACQS * LAGS, -1)
    design = design_matrix(pair_live)
    normal = jnp.dot(design.T, design, precision=lax.Precision.HIGHEST)
    factor = jnp.linalg.cholesky(normal)
    solved = jax.scipy.linalg.cho_solve((factor, True), design.T)
    flat_coef = jnp.concatenate([jnp.zeros((1, ACQS * LAGS), jnp.float32), solved], axis=0)
    displacement = jnp.dot(flat_coef, flat_obs, precision=lax.Precision.HIGHEST).reshape((ACQS,) + observed.shape[2:])
    disp_long = jnp.concatenate([displacement, jnp.zeros((LAGS,) + displacement.shape[1:], jnp.float32)], axis=0)
    later_disp = jnp.stack([disp_long[lag_index + 1:lag_index + 1 + ACQS] for lag_index in range(LAGS)], axis=1)
    live_all = (pair_live > 0)[:, :, None, None, None]
    residual = jnp.where(live_all, observed - (later_disp - displacement[:, None]), 0.0)
    return (displacement, residual)
```

```python
import functools

import jax
import jax.numpy as jnp
from jax import lax
from jax.experimental import pallas as pl
from jax.experimental.pallas import tpu as pltpu
from jax.sharding import PartitionSpec as P

MESH = pl.DeviceIdType.MESH
F32 = jnp.float32
BF16 = jnp.bfloat16
LOCAL = 4
BAND = 16
LAGS = 12
ROWS = 24
COLS = 128
GROUP = 48
CHUNK = 384
HALO = 10


def rem(a, n):
    return lax.rem(a + 4 * n, n)


def iota(shape, dim):
    return lax.broadcasted_iota(jnp.int32, shape, dim)


def split(value):
    high = value.astype(BF16)
    return high, (value - high.astype(F32)).astype(BF16)


def normal_matrix(live):
    n = live.shape[0]
    row, col = iota((n, n), 0), iota((n, n), 1)
    upper = jnp.zeros((n, n), F32)
    for k in range(LAGS):
        weight = jnp.where(live[:, k : k + 1] > 0, 1.0, 0.0)
        upper = upper + jnp.where(col == row + (k + 1), weight, 0.0)
    both = upper + upper.T
    degree = jnp.sum(both, axis=1, keepdims=True)
    full = jnp.where(row == col, degree, -both)
    grounded = jnp.where((row == 0) & (col == 0), 1.0, 0.0)
    return jnp.where((row == 0) | (col == 0), grounded, full)


def gauss_jordan(matrix):
    n = matrix.shape[0]
    row, col = iota((n, n), 0), iota((n, n), 1)

    def group(_, a):
        for s in range(8):
            pivot = 1.0 / a[s : s + 1, s : s + 1]
            scaled = jnp.where(col[:1] == s, pivot, a[s : s + 1, :] * pivot)
            update = jnp.where(col == s, 0.0, a) - a[:, s : s + 1] * scaled
            a = jnp.where(row == s, scaled, update)
        a = jnp.concatenate([a[8:], a[:8]], axis=0)
        return pltpu.roll(a, n - 8, axis=1)

    inverse = lax.fori_loop(0, n // 8, group, matrix)
    return jnp.where((row == 0) | (col == 0), 0.0, inverse)


def box_weights():
    source, out = iota((COLS, COLS), 0), iota((COLS, COLS), 1)
    own = (source >= out - HALO) & (source < out + HALO)
    side = jnp.where(source >= 4 * HALO, source - 4 * HALO, source)
    for step in (2, 1):
        side = jnp.where(side >= step * HALO, side - step * HALO, side)
    left = (source < 4 * HALO) & (out <= side)
    right = (source >= 4 * HALO) & (source < 8 * HALO) & (out >= side + COLS - HALO + 1)
    return jnp.concatenate(
        [jnp.where(own, 1.0, 0.0), jnp.where(left | right, 1.0, 0.0)], axis=0
    ).astype(BF16)


def kernel(
    n_acq, n_col,
    x_ref, live_ref, live_smem, disp_ref, res_ref,
    main, edges, packed, lhs_hi, lhs_lo, hx_hi, hx_lo, weights, ypad, scale, obs, rhs,
    inverse, p2_send, p2_recv, odd, sol, p3_send, p3_recv,
    own_sem, main_send, main_recv, edge_send, edge_recv, p2_ss, p2_rs, p3_ss, p3_rs,
):
    me, col = lax.axis_index("acq"), lax.axis_index("col")
    left, right = rem(col - 1, n_col), rem(col + 1, n_col)
    lane = iota((ROWS, COLS), 1)

    own = pltpu.make_async_copy(x_ref, main.at[pl.ds(0, LOCAL)], own_sem)
    own.start()

    barrier = pltpu.get_barrier_semaphore()

    @pl.loop(1, n_acq)
    def _(i):
        pl.semaphore_signal(barrier, inc=1, device_id=(rem(me + i, n_acq), col), device_id_type=MESH)

    for side in (left, right):

        @pl.loop(-3, 4)
        def _(i):
            pl.semaphore_signal(barrier, inc=1, device_id=(rem(me + i, n_acq), side), device_id_type=MESH)

    own.wait()
    to_right = jnp.zeros((ROWS, COLS), F32)
    to_left = jnp.zeros((ROWS, COLS), F32)
    for m in range(2):
        for i in range(LOCAL):
            base = 4 * HALO * m + HALO * i
            hit = (lane >= base) & (lane < base + HALO)
            value = main[i, m]
            to_right = jnp.where(hit, pltpu.roll(value, (base + HALO) % COLS, axis=1), to_right)
            to_left = jnp.where(hit, pltpu.roll(value, base, axis=1) if base else value, to_left)
    packed[0] = to_right
    packed[1] = to_left

    pl.semaphore_wait(barrier, n_acq - 1 + 14)

    copies = []
    for i in range(1, 4):
        copies.append(
            pltpu.make_async_remote_copy(
                x_ref, main.at[pl.ds(LOCAL * i, LOCAL)], main_send.at[i], main_recv.at[i],
                device_id=(rem(me - i, n_acq), col), device_id_type=MESH,
            )
        )
    for i in range(4):
        for side, target in ((0, right), (1, left)):
            copies.append(
                pltpu.make_async_remote_copy(
                    packed.at[side], edges.at[i, side], edge_send.at[i, side], edge_recv.at[i, side],
                    device_id=(rem(me - i, n_acq), target), device_id_type=MESH,
                )
            )
    for copy in copies:
        copy.start()

    inverse[...] = gauss_jordan(normal_matrix(live_ref[...]))
    weights[...] = box_weights()
    ypad[...] = jnp.zeros(ypad.shape, F32)
    rhs[...] = jnp.zeros(rhs.shape, F32)

    for copy in copies:
        copy.wait()

    keep_left = jnp.where(col > 0, 1.0, 0.0)
    keep_right = jnp.where(col < n_col - 1, 1.0, 0.0)
    in_left = lane < 4 * HALO
    in_right = (lane >= 4 * HALO) & (lane < 8 * HALO)
    real, imag = [], []
    for b in range(4):
        low, high = edges[b, 0] * keep_left, edges[b, 1] * keep_right
        real.append(jnp.where(in_left, low, jnp.where(in_right, pltpu.roll(high, 4 * HALO, axis=1), 0.0)))
        imag.append(jnp.where(in_left, pltpu.roll(low, COLS - 4 * HALO, axis=1), jnp.where(in_right, high, 0.0)))
    side_lane = jnp.where(lane >= 4 * HALO, lane - 4 * HALO, lane)

    def later(parts, lag):
        b, s = divmod(lag, 4)
        if s == 0:
            return parts[b]
        return jnp.where(
            side_lane < HALO * (4 - s),
            pltpu.roll(parts[b], COLS - HALO * s, axis=1),
            pltpu.roll(parts[b + 1], HALO * (4 - s), axis=1),
        )

    for k in range(LAGS):
        later_re, later_im = later(real, k + 1), later(imag, k + 1)
        cross = jnp.concatenate(
            [
                real[0] * later_re + imag[0] * later_im,
                imag[0] * later_re - real[0] * later_im,
            ],
            axis=0,
        )
        hx_hi[k], hx_lo[k] = split(cross)

    def slot_of(lanes, i):
        place = jnp.where(lanes >= 4 * HALO, lanes - 4 * HALO, lanes)
        return (place >= HALO * i) & (place < HALO * (i + 1)) & (lanes < 8 * HALO)

    for b in range(4):
        edge_power = real[b] * real[b] + imag[b] * imag[b]
        for h in range(2):
            parts, sides = [], []
            for i in (2 * h, 2 * h + 1):
                re, im = main[LOCAL * b + i, 0], main[LOCAL * b + i, 1]
                parts.append(re * re + im * im)
                sides.append(jnp.where(slot_of(lane, i), edge_power, 0.0))
            at = pl.ds((2 * b + h) * GROUP, GROUP)
            lhs_hi[at, :COLS], lhs_lo[at, :COLS] = split(jnp.concatenate(parts, axis=0))
            lhs_hi[at, COLS:], lhs_lo[at, COLS:] = split(jnp.concatenate(sides, axis=0))

    lane_wide = iota((GROUP, COLS), 1)
    slots = [jnp.where(slot_of(lane_wide, i), 1.0, 0.0).astype(BF16) for i in range(LOCAL)]

    @pl.loop(0, LAGS)
    def _(k):
        side_hi, side_lo = hx_hi[k], hx_lo[k]
        for e in range(LOCAL):
            re, im = main[e, 0], main[e, 1]
            re_j, im_j = main[e + k + 1, 0], main[e + k + 1, 1]
            cross = jnp.concatenate([re * re_j + im * im_j, im * re_j - re * im_j], axis=0)
            at = pl.ds(pl.multiple_of(CHUNK + k * (LOCAL * GROUP) + e * GROUP, 16), GROUP)
            lhs_hi[at, :COLS], lhs_lo[at, :COLS] = split(cross)
            lhs_hi[at, COLS:] = side_hi * slots[e]
            lhs_lo[at, COLS:] = side_lo * slots[e]

    def looked(chunk):
        at = pl.ds(pl.multiple_of(chunk * CHUNK, 16), CHUNK)
        by_cols = jnp.dot(lhs_hi[at, :], weights[...], preferred_element_type=F32)
        by_cols = by_cols + jnp.dot(lhs_lo[at, :], weights[...], preferred_element_type=F32)
        ypad[:, 8 : 8 + ROWS, :] = by_cols.reshape(CHUNK // ROWS, ROWS, COLS)

        def one(i):
            total = ypad[i, 6 : 6 + ROWS, :]
            for t in range(1, 5):
                total = total + ypad[i, 6 + t : 6 + t + ROWS, :]
            return total

        return one

    power = looked(0)
    for i in range(BAND):
        scale[i] = lax.rsqrt(power(i))

    @pl.loop(1, LAGS // 2 + 1)
    def _(chunk):
        one = looked(chunk)
        for half in range(2):
            k = 2 * chunk - 2 + half
            for e in range(LOCAL):
                live = jnp.where(live_smem[LOCAL * me + e, k] > 0, 1.0, 0.0)
                factor = scale[e] * scale[e + k + 1] * live
                for m in range(2):
                    value = one((half * LOCAL + e) * 2 + m) * factor
                    obs[e, k, m] = value
                    rhs[m, e] = rhs[m, e] - value
                    rhs[m, e + k + 1] = rhs[m, e + k + 1] + value

    for m in range(2):
        for j in range(BAND):
            p2_send[pl.ds(BAND * m + j, ROWS, stride=2 * BAND), :] = rhs[m, j]

    z = me // 4
    turn = me - 4 * z - lax.rem(z, 2)
    is_owner = (turn >= 0) & (turn < 3)
    row_me = 3 * z + turn
    first = rem(3 * z, ROWS)
    size = 2 * BAND

    @pl.loop(0, ROWS)
    def _(i):
        r = rem(first + i, ROWS)
        zr = r // 3
        target = 4 * zr + (r - 3 * zr) + lax.rem(zr, 2)

        @pl.when(target != me)
        def _():
            pltpu.make_async_remote_copy(
                p2_send.at[pl.ds(pl.multiple_of(r * size, 8), size)],
                p2_recv.at[pl.ds(pl.multiple_of(me * size, 8), size)],
                p2_ss, p2_rs, device_id=(target, col), device_id_type=MESH,
            ).start()

    def wait(ref, blocks, sem):
        part = ref.at[pl.ds(0, blocks * size)]
        pltpu.make_async_copy(part, part, sem).wait()

    @pl.when(is_owner)
    def _():
        p2_recv[pl.ds(pl.multiple_of(me * size, 8), size), :] = p2_send[
            pl.ds(pl.multiple_of(row_me * size, 8), size), :
        ]
        wait(p2_recv, n_acq - 1, p2_rs)
        sums = []
        for m in range(2):

            def part(a, h):
                at = a * size + m * BAND + 8 * h
                return p2_recv[at : at + 8, :]

            odd[m, 0:8, :] = jnp.zeros((8, COLS), F32)
            for v in range(16):
                value = part(2 * v + 1, 0)
                if v:
                    value = value + part(2 * v - 1, 1)
                odd[m, 8 * v + 8 : 8 * v + 16, :] = value
            even = []
            for v in range(16):
                value = part(2 * v, 0)
                if v:
                    value = value + part(2 * v - 2, 1)
                even.append(value)
            sums.append(jnp.concatenate(even, axis=0) + odd[m, 4 : 4 + 128, :])
        solved = jnp.dot(
            inverse[...], jnp.concatenate(sums, axis=1),
            precision=lax.Precision.HIGHEST, preferred_element_type=F32,
        )
        for m in range(2):
            sol[m, 0:128, :] = solved[:, m * COLS : (m + 1) * COLS]
            sol[m, 128:144, :] = jnp.zeros((16, COLS), F32)
        for a in range(32):
            for m in range(2):
                at = a * size + m * BAND
                p3_send[at : at + BAND, :] = sol[m, 4 * a : 4 * a + BAND, :]

        @pl.loop(1, n_acq)
        def _(i):
            target = rem(me + i, n_acq)
            pltpu.make_async_remote_copy(
                p3_send.at[pl.ds(pl.multiple_of(target * size, 8), size)],
                p3_recv.at[pl.ds(pl.multiple_of(row_me * size, 8), size)],
                p3_ss, p3_rs, device_id=(target, col), device_id_type=MESH,
            ).start()

        p3_recv[pl.ds(pl.multiple_of(row_me * size, 8), size), :] = p3_send[
            pl.ds(pl.multiple_of(me * size, 8), size), :
        ]
        wait(p2_send, ROWS - 1, p2_ss)
        wait(p3_recv, ROWS - 1, p3_rs)
        wait(p3_send, n_acq - 1, p3_ss)

    @pl.when(jnp.logical_not(is_owner))
    def _():
        wait(p2_send, ROWS, p2_ss)
        wait(p3_recv, ROWS, p3_rs)

    for m in range(2):
        for j in range(BAND):
            rhs[m, j] = p3_recv[pl.ds(BAND * m + j, ROWS, stride=2 * BAND), :]
    for e in range(LOCAL):
        for m in range(2):
            disp_ref[e, m] = rhs[m, e]

    @pl.loop(0, LAGS)
    def _(k):
        for e in range(LOCAL):
            live = jnp.where(live_smem[LOCAL * me + e, k] > 0, 1.0, 0.0)
            for m in range(2):
                res_ref[e, k, m] = obs[e, k, m] - (rhs[m, e + k + 1] - rhs[m, e]) * live


def per_device(n_acq, n_col, samples, pair_live):
    vmem = pltpu.VMEM
    rows_all = CHUNK + LAGS * LOCAL * GROUP
    return pl.pallas_call(
        functools.partial(kernel, n_acq, n_col),
        out_shape=(
            jax.ShapeDtypeStruct((LOCAL, 2, ROWS, COLS), F32),
            jax.ShapeDtypeStruct((LOCAL, LAGS, 2, ROWS, COLS), F32),
        ),
        in_specs=[
            pl.BlockSpec(memory_space=pl.ANY),
            pl.BlockSpec(memory_space=pltpu.VMEM),
            pl.BlockSpec(memory_space=pltpu.SMEM),
        ],
        out_specs=(pl.BlockSpec(memory_space=pltpu.VMEM), pl.BlockSpec(memory_space=pltpu.VMEM)),
        scratch_shapes=[
            vmem((BAND, 2, ROWS, COLS), F32),
            vmem((4, 2, ROWS, COLS), F32),
            vmem((2, ROWS, COLS), F32),
            vmem((rows_all, 2 * COLS), BF16),
            vmem((rows_all, 2 * COLS), BF16),
            vmem((LAGS, GROUP, COLS), BF16),
            vmem((LAGS, GROUP, COLS), BF16),
            vmem((2 * COLS, COLS), BF16),
            vmem((CHUNK // ROWS, 40, COLS), F32),
            vmem((BAND, ROWS, COLS), F32),
            vmem((LOCAL, LAGS, 2, ROWS, COLS), F32),
            vmem((2, BAND, ROWS, COLS), F32),
            vmem((128, 128), F32),
            vmem((ROWS * 2 * BAND, COLS), F32),
            vmem((n_acq * 2 * BAND, COLS), F32),
            vmem((2, 136, COLS), F32),
            vmem((2, 144, COLS), F32),
            vmem((n_acq * 2 * BAND, COLS), F32),
            vmem((ROWS * 2 * BAND, COLS), F32),
            pltpu.SemaphoreType.DMA,
            pltpu.SemaphoreType.DMA((4,)),
            pltpu.SemaphoreType.DMA((4,)),
            pltpu.SemaphoreType.DMA((4, 2)),
            pltpu.SemaphoreType.DMA((4, 2)),
            pltpu.SemaphoreType.DMA,
            pltpu.SemaphoreType.DMA,
            pltpu.SemaphoreType.DMA,
            pltpu.SemaphoreType.DMA,
        ],
        compiler_params=pltpu.CompilerParams(
            collective_id=0, has_side_effects=True, vmem_limit_bytes=32 * 1024 * 1024
        ),
    )(samples, pair_live, pair_live)


def solution(mesh):
    return jax.shard_map(
        functools.partial(per_device, mesh.shape["acq"], mesh.shape["col"]),
        mesh=mesh,
        in_specs=(P("acq", None, None, "col"), P()),
        out_specs=(P("acq", None, None, "col"), P("acq", None, None, None, "col")),
        check_vma=False,
    )
```

```python
import functools

import jax
import jax.numpy as jnp
from jax import lax
from jax.experimental import pallas as pl
from jax.experimental.pallas import tpu as pltpu
from jax.sharding import PartitionSpec as P

MESH = pl.DeviceIdType.MESH
F32 = jnp.float32
BF16 = jnp.bfloat16
LOCAL = 4
BAND = 16
LAGS = 12
ROWS = 24
COLS = 128
GROUP = 48
CHUNK = 384
HALO = 10
WINDOW = 2 * BAND
WIDE = 40


def rem(a, n):
    return lax.rem(a + 4 * n, n)


def iota(shape, dim):
    return lax.broadcasted_iota(jnp.int32, shape, dim)


def split(value):
    high = value.astype(BF16)
    return high, (value - high.astype(F32)).astype(BF16)


def normal_matrix(live):
    n = live.shape[1]
    row, col = iota((n, n), 0), iota((n, n), 1)
    lower = jnp.zeros((n, n), F32)
    for k in range(LAGS):
        weight = jnp.where(live[k : k + 1, :] > 0, 1.0, 0.0)
        lower = lower + jnp.where(row == col + (k + 1), weight, 0.0)
    both = lower + lower.T
    degree = jnp.sum(both, axis=1, keepdims=True)
    full = jnp.where(row == col, degree, -both)
    grounded = jnp.where((row == 0) & (col == 0), 1.0, 0.0)
    return jnp.where((row == 0) | (col == 0), grounded, full)


def eliminate(matrix, groups):
    n = matrix.shape[0]
    row, col = iota((n, n), 0), iota((n, n), 1)

    def group(_, a):
        for s in range(8):
            pivot = 1.0 / a[s : s + 1, s : s + 1]
            scaled = jnp.where(col[:1] == s, pivot, a[s : s + 1, :] * pivot)
            update = jnp.where(col == s, 0.0, a) - a[:, s : s + 1] * scaled
            a = jnp.where(row == s, scaled, update)
        a = jnp.concatenate([a[8:], a[:8]], axis=0)
        return pltpu.roll(a, n - 8, axis=1)

    return lax.fori_loop(0, groups, group, matrix)


def ungrounded(inverse):
    row, col = iota(inverse.shape, 0), iota(inverse.shape, 1)
    return jnp.where((row == 0) | (col == 0), 0.0, inverse)


def box_weights():
    source, out = iota((COLS, COLS), 0), iota((COLS, COLS), 1)
    own = (source >= out - HALO) & (source < out + HALO)
    side = jnp.where(source >= 4 * HALO, source - 4 * HALO, source)
    for step in (2, 1):
        side = jnp.where(side >= step * HALO, side - step * HALO, side)
    left = (source < 4 * HALO) & (out <= side)
    right = (source >= 4 * HALO) & (source < 8 * HALO) & (out >= side + COLS - HALO + 1)
    return jnp.concatenate(
        [jnp.where(own, 1.0, 0.0), jnp.where(left | right, 1.0, 0.0)], axis=0
    ).astype(BF16)


def kernel(
    n_acq, n_col,
    x_ref, live_ref, live_smem, disp_ref, res_ref,
    main, edges, packed, lhs_hi, lhs_lo, hx_hi, hx_lo, weights, ypad, scale, obs, rhs,
    inverse, p2_send, p2_sib, p2_chip, p2_recv, sol, p3_recv,
    own_sem, main_send, main_recv, edge_send, edge_recv, sib_ss, sib_rs, p2_ss, p2_rs, p3_ss, p3_rs, fw_ss, fw_rs,
):
    me, col = lax.axis_index("acq"), lax.axis_index("col")
    left, right = rem(col - 1, n_col), rem(col + 1, n_col)
    lane = iota((ROWS, COLS), 1)

    own = pltpu.make_async_copy(x_ref, main.at[pl.ds(0, LOCAL)], own_sem)
    own.start()

    barrier = pltpu.get_barrier_semaphore()

    def greet(target):
        pl.semaphore_signal(barrier, inc=1, device_id=(target, col), device_id_type=MESH)

    for i in (1, -1, 3, -3):
        greet(rem(me + i, n_acq))

    @pl.loop(1, n_acq // 2)
    def _(i):
        greet(rem(me + 2 * i, n_acq))

    for side in (left, right):

        @pl.loop(-3, 4)
        def _(i):
            pl.semaphore_signal(barrier, inc=1, device_id=(rem(me + i, n_acq), side), device_id_type=MESH)

    own.wait()
    to_right = jnp.zeros((ROWS, COLS), F32)
    to_left = jnp.zeros((ROWS, COLS), F32)
    for m in range(2):
        for i in range(LOCAL):
            base = 4 * HALO * m + HALO * i
            hit = (lane >= base) & (lane < base + HALO)
            value = main[i, m]
            to_right = jnp.where(hit, pltpu.roll(value, (base + HALO) % COLS, axis=1), to_right)
            to_left = jnp.where(hit, pltpu.roll(value, base, axis=1) if base else value, to_left)
    packed[0] = to_right
    packed[1] = to_left

    pl.semaphore_wait(barrier, 4 + n_acq // 2 - 1 + 14)

    copies = []
    for i in range(1, 4):
        copies.append(
            pltpu.make_async_remote_copy(
                x_ref, main.at[pl.ds(LOCAL * i, LOCAL)], main_send.at[i], main_recv.at[i],
                device_id=(rem(me - i, n_acq), col), device_id_type=MESH,
            )
        )
    for i in range(4):
        for side, target in ((0, right), (1, left)):
            copies.append(
                pltpu.make_async_remote_copy(
                    packed.at[side], edges.at[i, side], edge_send.at[i, side], edge_recv.at[i, side],
                    device_id=(rem(me - i, n_acq), target), device_id_type=MESH,
                )
            )
    for copy in copies:
        copy.start()

    inverse[...] = eliminate(normal_matrix(live_ref[...]), 8)
    weights[...] = box_weights()
    ypad[...] = jnp.zeros(ypad.shape, F32)
    rhs[...] = jnp.zeros(rhs.shape, F32)

    for copy in copies:
        copy.wait()

    keep_left = jnp.where(col > 0, 1.0, 0.0)
    keep_right = jnp.where(col < n_col - 1, 1.0, 0.0)
    in_left = lane < 4 * HALO
    in_right = (lane >= 4 * HALO) & (lane < 8 * HALO)
    real, imag = [], []
    for b in range(4):
        low, high = edges[b, 0] * keep_left, edges[b, 1] * keep_right
        real.append(jnp.where(in_left, low, jnp.where(in_right, pltpu.roll(high, 4 * HALO, axis=1), 0.0)))
        imag.append(jnp.where(in_left, pltpu.roll(low, COLS - 4 * HALO, axis=1), jnp.where(in_right, high, 0.0)))
    side_lane = jnp.where(lane >= 4 * HALO, lane - 4 * HALO, lane)

    def later(parts, lag):
        b, s = divmod(lag, 4)
        if s == 0:
            return parts[b]
        return jnp.where(
            side_lane < HALO * (4 - s),
            pltpu.roll(parts[b], COLS - HALO * s, axis=1),
            pltpu.roll(parts[b + 1], HALO * (4 - s), axis=1),
        )

    for k in range(LAGS):
        later_re, later_im = later(real, k + 1), later(imag, k + 1)
        cross = jnp.concatenate(
            [
                real[0] * later_re + imag[0] * later_im,
                imag[0] * later_re - real[0] * later_im,
            ],
            axis=0,
        )
        hx_hi[k], hx_lo[k] = split(cross)

    def slot_of(lanes, i):
        place = jnp.where(lanes >= 4 * HALO, lanes - 4 * HALO, lanes)
        return (place >= HALO * i) & (place < HALO * (i + 1)) & (lanes < 8 * HALO)

    for b in range(4):
        edge_power = real[b] * real[b] + imag[b] * imag[b]
        for h in range(2):
            parts, sides = [], []
            for i in (2 * h, 2 * h + 1):
                re, im = main[LOCAL * b + i, 0], main[LOCAL * b + i, 1]
                parts.append(re * re + im * im)
                sides.append(jnp.where(slot_of(lane, i), edge_power, 0.0))
            at = pl.ds((2 * b + h) * GROUP, GROUP)
            lhs_hi[at, :COLS], lhs_lo[at, :COLS] = split(jnp.concatenate(parts, axis=0))
            lhs_hi[at, COLS:], lhs_lo[at, COLS:] = split(jnp.concatenate(sides, axis=0))

    lane_wide = iota((GROUP, COLS), 1)
    slots = [jnp.where(slot_of(lane_wide, i), 1.0, 0.0).astype(BF16) for i in range(LOCAL)]

    @pl.loop(0, LAGS)
    def _(k):
        side_hi, side_lo = hx_hi[k], hx_lo[k]
        for e in range(LOCAL):
            re, im = main[e, 0], main[e, 1]
            re_j, im_j = main[e + k + 1, 0], main[e + k + 1, 1]
            cross = jnp.concatenate([re * re_j + im * im_j, im * re_j - re * im_j], axis=0)
            at = pl.ds(pl.multiple_of(CHUNK + k * (LOCAL * GROUP) + e * GROUP, 16), GROUP)
            lhs_hi[at, :COLS], lhs_lo[at, :COLS] = split(cross)
            lhs_hi[at, COLS:] = side_hi * slots[e]
            lhs_lo[at, COLS:] = side_lo * slots[e]

    def looked(chunk):
        at = pl.ds(pl.multiple_of(chunk * CHUNK, 16), CHUNK)
        by_cols = jnp.dot(lhs_hi[at, :], weights[...], preferred_element_type=F32)
        by_cols = by_cols + jnp.dot(lhs_lo[at, :], weights[...], preferred_element_type=F32)
        ypad[:, 8 : 8 + ROWS, :] = by_cols.reshape(CHUNK // ROWS, ROWS, COLS)

        def one(i):
            total = ypad[i, 6 : 6 + ROWS, :]
            for t in range(1, 5):
                total = total + ypad[i, 6 + t : 6 + t + ROWS, :]
            return total

        return one

    power = looked(0)
    for i in range(BAND):
        scale[i] = lax.rsqrt(power(i))

    @pl.loop(1, LAGS // 2 + 1)
    def _(chunk):
        one = looked(chunk)
        for half in range(2):
            k = 2 * chunk - 2 + half
            for e in range(LOCAL):
                live = jnp.where(live_smem[k, LOCAL * me + e] > 0, 1.0, 0.0)
                factor = scale[e] * scale[e + k + 1] * live
                for m in range(2):
                    value = one((half * LOCAL + e) * 2 + m) * factor
                    obs[e, k, m] = value
                    rhs[m, e] = rhs[m, e] - value
                    rhs[m, e + k + 1] = rhs[m, e + k + 1] + value

    for m in range(2):
        for j in range(BAND):
            p2_send[pl.ds(8 * (j // 4) + 4 * m + j % 4, ROWS, stride=WINDOW), :] = rhs[m, j]

    core = lax.rem(me, 2)
    chip = me // 2
    z, x = chip // 2, lax.rem(chip, 2)
    sibling = me + 1 - 2 * core
    planes = n_acq // 4
    half = ROWS // 2

    def place(zt, xt):
        both = lax.rem(zt, 2) == core
        return both | (xt == lax.rem(zt // 2 + core, 2)), 3 * (zt // 2) + jnp.where(both, xt, 2)

    def plane(turn):
        away = (planes - turn) // 2
        return rem(jnp.where(lax.rem(turn, 2) == 1, z + away, z - away), planes)

    to_sibling = pltpu.make_async_remote_copy(
        p2_send.at[pl.ds(pl.multiple_of((1 - core) * half * WINDOW, 8), half * WINDOW)],
        p2_sib, sib_ss, sib_rs, device_id=(sibling, col), device_id_type=MESH,
    )
    to_sibling.start()
    to_sibling.wait()
    mine_first = core == 0

    @pl.loop(0, half)
    def _(u):
        first, second = [], []
        for g in range(4):
            mine = p2_send[pl.ds(pl.multiple_of((core * half + u) * WINDOW + 8 * g, 8), 8), :]
            other = p2_sib[pl.ds(pl.multiple_of(u * WINDOW + 8 * g, 8), 8), :]
            first.append(jnp.where(mine_first, mine, other))
            second.append(jnp.where(mine_first, other, mine))
        total = [first[0]] + [first[g] + second[g - 1] for g in range(1, 4)] + [second[3]]
        p2_chip[pl.ds(pl.multiple_of(u * WIDE, 8), WIDE), :] = jnp.concatenate(total, axis=0)

    is_owner, row_me = place(z, x)

    @pl.loop(0, planes)
    def _(turn):
        zt = plane(turn)
        for xt in range(2):
            owns, u = place(zt, xt)
            target = 4 * zt + 2 * xt + core

            @pl.when(owns & (target != me))
            def _():
                pltpu.make_async_remote_copy(
                    p2_chip.at[pl.ds(pl.multiple_of(u * WIDE, 8), WIDE)],
                    p2_recv.at[pl.ds(pl.multiple_of(chip * WIDE, 8), WIDE)],
                    p2_ss, p2_rs, device_id=(target, col), device_id_type=MESH,
                ).start()

    def wait(ref, blocks, sem):
        part = ref.at[pl.ds(0, blocks * WIDE)]
        pltpu.make_async_copy(part, part, sem).wait()

    chips = n_acq // 2
    row_at = pl.multiple_of((core * half + row_me) * WIDE, 8)

    @pl.when(is_owner)
    def _():
        inverse[...] = ungrounded(eliminate(inverse[...], 8))
        p2_recv[pl.ds(pl.multiple_of(chip * WIDE, 8), WIDE), :] = p2_chip[
            pl.ds(pl.multiple_of(row_me * WIDE, 8), WIDE), :
        ]
        wait(p2_recv, chips - 1, p2_rs)
        groups = []
        for b in range(n_acq):
            total = None
            for g in range(b % 2, 5, 2):
                c = (b - g) // 2
                if c >= 0:
                    part = p2_recv[c * WIDE + 8 * g : c * WIDE + 8 * g + 8, :]
                    total = part if total is None else total + part
            groups.append(total)
        low = iota((8, COLS), 0) < 4
        first, second = [], []
        for v in range(n_acq // 2):
            one, two = groups[2 * v], groups[2 * v + 1]
            first.append(jnp.where(low, one, pltpu.roll(two, 4, axis=0)))
            second.append(jnp.where(low, pltpu.roll(one, 4, axis=0), two))
        sums = jnp.concatenate(
            [jnp.concatenate(first, axis=0), jnp.concatenate(second, axis=0)], axis=1
        )
        solved = jnp.dot(
            inverse[...], sums, precision=lax.Precision.HIGHEST, preferred_element_type=F32
        )
        for v in range(n_acq // 2):
            one, two = solved[8 * v : 8 * v + 8, :COLS], solved[8 * v : 8 * v + 8, COLS:]
            sol[16 * v : 16 * v + 8, :] = jnp.where(low, one, pltpu.roll(two, 4, axis=0))
            sol[16 * v + 8 : 16 * v + 16, :] = jnp.where(low, pltpu.roll(one, 4, axis=0), two)
        sol[8 * n_acq :, :] = jnp.zeros((24, COLS), F32)

        @pl.loop(0, planes)
        def _(turn):
            zt = plane(turn)
            for xt in range(2):
                target = 4 * zt + 2 * xt + core

                @pl.when(target != me)
                def _():
                    pltpu.make_async_remote_copy(
                        sol.at[pl.ds(pl.multiple_of((2 * zt + xt) * 16, 8), WIDE)],
                        p3_recv.at[pl.ds(row_at, WIDE)],
                        p3_ss, p3_rs, device_id=(target, col), device_id_type=MESH,
                    ).start()

        p3_recv[pl.ds(row_at, WIDE), :] = sol[pl.ds(pl.multiple_of(chip * 16, 8), WIDE), :]
        wait(p3_recv, half - 1, p3_rs)

    @pl.when(jnp.logical_not(is_owner))
    def _():
        wait(p3_recv, half, p3_rs)

    own_half = pl.ds(pl.multiple_of(core * half * WIDE, 8), half * WIDE)
    forward = pltpu.make_async_remote_copy(
        p3_recv.at[own_half], p3_recv.at[own_half], fw_ss, fw_rs,
        device_id=(sibling, col), device_id_type=MESH,
    )
    forward.start()

    @pl.when(is_owner)
    def _():
        wait(p2_chip, half - 1, p2_ss)
        wait(p2_recv, chips - 1, p3_ss)

    @pl.when(jnp.logical_not(is_owner))
    def _():
        wait(p2_chip, half, p2_ss)

    forward.wait()

    for m in range(2):
        for j in range(BAND):
            rhs[m, j] = p3_recv[pl.ds(8 * core + 8 * (j // 4) + 4 * m + j % 4, ROWS, stride=WIDE), :]
    for e in range(LOCAL):
        for m in range(2):
            disp_ref[e, m] = rhs[m, e]

    @pl.loop(0, LAGS)
    def _(k):
        for e in range(LOCAL):
            live = jnp.where(live_smem[k, LOCAL * me + e] > 0, 1.0, 0.0)
            for m in range(2):
                res_ref[e, k, m] = obs[e, k, m] - (rhs[m, e + k + 1] - rhs[m, e]) * live


def per_device(n_acq, n_col, samples, pair_live):
    vmem = pltpu.VMEM
    rows_all = CHUNK + LAGS * LOCAL * GROUP
    return pl.pallas_call(
        functools.partial(kernel, n_acq, n_col),
        out_shape=(
            jax.ShapeDtypeStruct((LOCAL, 2, ROWS, COLS), F32),
            jax.ShapeDtypeStruct((LOCAL, LAGS, 2, ROWS, COLS), F32),
        ),
        in_specs=[
            pl.BlockSpec(memory_space=pltpu.HBM),
            pl.BlockSpec(memory_space=pltpu.VMEM),
            pl.BlockSpec(memory_space=pltpu.SMEM),
        ],
        out_specs=(pl.BlockSpec(memory_space=pltpu.VMEM), pl.BlockSpec(memory_space=pltpu.VMEM)),
        scratch_shapes=[
            vmem((BAND, 2, ROWS, COLS), F32),
            vmem((4, 2, ROWS, COLS), F32),
            vmem((2, ROWS, COLS), F32),
            vmem((rows_all, 2 * COLS), BF16),
            vmem((rows_all, 2 * COLS), BF16),
            vmem((LAGS, GROUP, COLS), BF16),
            vmem((LAGS, GROUP, COLS), BF16),
            vmem((2 * COLS, COLS), BF16),
            vmem((CHUNK // ROWS, 40, COLS), F32),
            vmem((BAND, ROWS, COLS), F32),
            vmem((LOCAL, LAGS, 2, ROWS, COLS), F32),
            vmem((2, BAND, ROWS, COLS), F32),
            vmem((128, 128), F32),
            vmem((ROWS * WINDOW, COLS), F32),
            vmem((ROWS // 2 * WINDOW, COLS), F32),
            vmem((ROWS // 2 * WIDE, COLS), F32),
            vmem((n_acq // 2 * WIDE, COLS), F32),
            vmem((8 * n_acq + 24, COLS), F32),
            vmem((ROWS * WIDE, COLS), F32),
            pltpu.SemaphoreType.DMA,
            pltpu.SemaphoreType.DMA((4,)),
            pltpu.SemaphoreType.DMA((4,)),
            pltpu.SemaphoreType.DMA((4, 2)),
            pltpu.SemaphoreType.DMA((4, 2)),
        ] + [pltpu.SemaphoreType.DMA] * 8,
        compiler_params=pltpu.CompilerParams(
            collective_id=0, has_side_effects=True, vmem_limit_bytes=32 * 1024 * 1024
        ),
    )(samples, pair_live.T, pair_live.T)


def solution(mesh):
    return jax.shard_map(
        functools.partial(per_device, mesh.shape["acq"], mesh.shape["col"]),
        mesh=mesh,
        in_specs=(P("acq", None, None, "col"), P()),
        out_specs=(P("acq", None, None, "col"), P("acq", None, None, None, "col")),
        check_vma=False,
    )
```

```python
import functools

import jax
import jax.numpy as jnp
from jax import lax
from jax.experimental import pallas as pl
from jax.experimental.pallas import tpu as pltpu
from jax.sharding import PartitionSpec as P

MESH = pl.DeviceIdType.MESH
F32 = jnp.float32
BF16 = jnp.bfloat16
LOCAL = 4
BAND = 16
LAGS = 12
ROWS = 24
COLS = 128
GROUP = 48
FIRST_GROUPS = 8
HALO = 10
WINDOW = 2 * BAND
WIDE = 40


def rem(a, n):
    return lax.rem(a + 4 * n, n)


def iota(shape, dim):
    return lax.broadcasted_iota(jnp.int32, shape, dim)


def split(value):
    high = value.astype(BF16)
    return high, (value - high.astype(F32)).astype(BF16)


def normal_matrix(live):
    n = live.shape[1]
    row, col = iota((n, n), 0), iota((n, n), 1)
    lower = jnp.zeros((n, n), F32)
    for k in range(LAGS):
        weight = jnp.where(live[k : k + 1, :] > 0, 1.0, 0.0)
        lower = lower + jnp.where(row == col + (k + 1), weight, 0.0)
    both = lower + lower.T
    degree = jnp.sum(both, axis=1, keepdims=True)
    full = jnp.where(row == col, degree, -both)
    grounded = jnp.where((row == 0) & (col == 0), 1.0, 0.0)
    return jnp.where((row == 0) | (col == 0), grounded, full)


def eliminate(matrix, groups):
    n = matrix.shape[0]
    lane, top = iota((1, n), 1), iota((8, n), 0)

    def group(_, a):
        for s in range(8):
            pivot = 1.0 / a[s : s + 1, s : s + 1]
            hit = lane == s
            scaled = jnp.where(hit, pivot, a[s : s + 1, :] * pivot)
            a = jnp.where(hit, 0.0, a) - a[:, s : s + 1] * scaled
            a = jnp.concatenate([jnp.where(top == s, scaled, a[:8]), a[8:]], axis=0)
        a = jnp.concatenate([a[8:], a[:8]], axis=0)
        return pltpu.roll(a, n - 8, axis=1)

    return lax.fori_loop(0, groups, group, matrix)


def ungrounded(inverse):
    row, col = iota(inverse.shape, 0), iota(inverse.shape, 1)
    return jnp.where((row == 0) | (col == 0), 0.0, inverse)


def box_weights():
    source, out = iota((COLS, COLS), 0), iota((COLS, COLS), 1)
    own = (source >= out - HALO) & (source < out + HALO)
    side = jnp.where(source >= 4 * HALO, source - 4 * HALO, source)
    for step in (2, 1):
        side = jnp.where(side >= step * HALO, side - step * HALO, side)
    left = (source < 4 * HALO) & (out <= side)
    right = (source >= 4 * HALO) & (source < 8 * HALO) & (out >= side + COLS - HALO + 1)
    return jnp.concatenate(
        [jnp.where(own, 1.0, 0.0), jnp.where(left | right, 1.0, 0.0)], axis=0
    ).astype(BF16)


def kernel(
    n_acq, n_col,
    x_ref, live_hbm, disp_ref, res_ref,
    main, edges, packed, lhs_hi, lhs_lo, weights, ypad, scale, obs, rhs,
    inverse, p2_send, p2_sib, p2_chip, p2_recv, sol, p3_recv,
    live_ref, live_smem, own_sem, live_sem, main_send, main_recv, edge_send, edge_recv, sib_ss, sib_rs, p2_ss, p2_rs, p3_ss, p3_rs, fw_ss, fw_rs,
):
    me, col = lax.axis_index("acq"), lax.axis_index("col")
    left, right = rem(col - 1, n_col), rem(col + 1, n_col)
    lane = iota((ROWS, COLS), 1)

    own = pltpu.make_async_copy(x_ref, main.at[pl.ds(0, LOCAL)], own_sem)
    own.start()
    lives = [
        pltpu.make_async_copy(live_hbm, live_ref, live_sem.at[0]),
        pltpu.make_async_copy(live_hbm, live_smem, live_sem.at[1]),
    ]
    for copy in lives:
        copy.start()

    barrier = pltpu.get_barrier_semaphore()

    def greet(target):
        pl.semaphore_signal(barrier, inc=1, device_id=(target, col), device_id_type=MESH)

    for i in (1, -1, 3, -3):
        greet(rem(me + i, n_acq))

    @pl.loop(1, n_acq // 2)
    def _(i):
        greet(rem(me + 2 * i, n_acq))

    for side in (left, right):

        @pl.loop(-3, 4)
        def _(i):
            pl.semaphore_signal(barrier, inc=1, device_id=(rem(me + i, n_acq), side), device_id_type=MESH)

    own.wait()
    to_right = jnp.zeros((ROWS, COLS), F32)
    to_left = jnp.zeros((ROWS, COLS), F32)
    for m in range(2):
        for i in range(LOCAL):
            base = 4 * HALO * m + HALO * i
            hit = (lane >= base) & (lane < base + HALO)
            value = main[i, m]
            to_right = jnp.where(hit, pltpu.roll(value, (base + HALO) % COLS, axis=1), to_right)
            to_left = jnp.where(hit, pltpu.roll(value, base, axis=1) if base else value, to_left)
    packed[0] = to_right
    packed[1] = to_left

    pl.semaphore_wait(barrier, 4 + n_acq // 2 - 1 + 14)

    blocks, sides = [], []
    for i in range(1, 4):
        blocks.append(
            pltpu.make_async_remote_copy(
                x_ref, main.at[pl.ds(LOCAL * i, LOCAL)], main_send.at[i], main_recv.at[i],
                device_id=(rem(me - i, n_acq), col), device_id_type=MESH,
            )
        )
    for i in range(4):
        for side, target in ((0, right), (1, left)):
            sides.append(
                pltpu.make_async_remote_copy(
                    packed.at[side], edges.at[i, side], edge_send.at[i, side], edge_recv.at[i, side],
                    device_id=(rem(me - i, n_acq), target), device_id_type=MESH,
                )
            )
    for i in range(4):
        if i:
            blocks[i - 1].start()
        sides[2 * i].start()
        sides[2 * i + 1].start()

    for copy in lives:
        copy.wait()
    inverse[...] = eliminate(normal_matrix(live_ref[...]), FIRST_GROUPS)
    weights[...] = box_weights()
    ypad[...] = jnp.zeros(ypad.shape, F32)
    rhs[...] = jnp.zeros(rhs.shape, F32)

    keep_left = jnp.where(col > 0, 1.0, 0.0)
    keep_right = jnp.where(col < n_col - 1, 1.0, 0.0)
    in_left = lane < 4 * HALO
    in_right = (lane >= 4 * HALO) & (lane < 8 * HALO)

    def slot_of(lanes, i):
        place = jnp.where(lanes >= 4 * HALO, lanes - 4 * HALO, lanes)
        return (place >= HALO * i) & (place < HALO * (i + 1)) & (lanes < 8 * HALO)

    lane_wide = iota((GROUP, COLS), 1)
    slots = [jnp.where(slot_of(lane_wide, i), 1.0, 0.0).astype(BF16) for i in range(LOCAL)]

    def turned(value, by):
        return pltpu.roll(value, by % COLS, axis=1) if by % COLS else value

    at_row = 0
    for b in range(4):
        if b:
            blocks[b - 1].wait_recv()
        sides[2 * b].wait_recv()
        sides[2 * b + 1].wait_recv()
        low, high = edges[b, 0] * keep_left, edges[b, 1] * keep_right
        real = jnp.where(in_left, low, jnp.where(in_right, turned(high, 4 * HALO), 0.0))
        imag = jnp.where(in_left, turned(low, -4 * HALO), jnp.where(in_right, high, 0.0))
        if b == 0:
            own_real, own_imag = real, imag
        first_row = at_row
        edge_power = real * real + imag * imag
        for h in range(2):
            parts, outer = [], []
            for i in (2 * h, 2 * h + 1):
                re, im = main[LOCAL * b + i, 0], main[LOCAL * b + i, 1]
                parts.append(re * re + im * im)
                outer.append(jnp.where(slot_of(lane, i), edge_power, 0.0))
            at = pl.ds(at_row, GROUP)
            lhs_hi[at, :COLS], lhs_lo[at, :COLS] = split(jnp.concatenate(parts, axis=0))
            lhs_hi[at, COLS:], lhs_lo[at, COLS:] = split(jnp.concatenate(outer, axis=0))
            at_row += GROUP
        pairs = []
        for t in range(-3, 4):
            lag = 4 * b + t
            if not 1 <= lag <= LAGS:
                continue
            later_re, later_im = turned(real, -HALO * t), turned(imag, -HALO * t)
            side_hi, side_lo = split(
                jnp.concatenate(
                    [
                        own_real * later_re + own_imag * later_im,
                        own_imag * later_re - own_real * later_im,
                    ],
                    axis=0,
                )
            )
            for e in range(max(0, -t), min(LOCAL, LOCAL - t)):
                re, im = main[e, 0], main[e, 1]
                re_j, im_j = main[e + lag, 0], main[e + lag, 1]
                cross = jnp.concatenate([re * re_j + im * im_j, im * re_j - re * im_j], axis=0)
                at = pl.ds(at_row, GROUP)
                lhs_hi[at, :COLS], lhs_lo[at, :COLS] = split(cross)
                lhs_hi[at, COLS:] = side_hi * slots[e]
                lhs_lo[at, COLS:] = side_lo * slots[e]
                at_row += GROUP
                pairs.append((e, lag))

        at = pl.ds(first_row, at_row - first_row)
        by_cols = jnp.dot(lhs_hi[at, :], weights[...], preferred_element_type=F32)
        by_cols = by_cols + jnp.dot(lhs_lo[at, :], weights[...], preferred_element_type=F32)
        first, count = first_row // ROWS, (at_row - first_row) // ROWS
        ypad[pl.ds(first, count), 8 : 8 + ROWS, :] = by_cols.reshape(count, ROWS, COLS)

        def looked(i):
            total = ypad[i, 6 : 6 + ROWS, :]
            for step in range(1, 5):
                total = total + ypad[i, 6 + step : 6 + step + ROWS, :]
            return total

        for i in range(LOCAL):
            scale[LOCAL * b + i] = lax.rsqrt(looked(first + i))
        for place, (e, lag) in enumerate(pairs):
            live = jnp.where(live_smem[lag - 1, LOCAL * me + e] > 0, 1.0, 0.0)
            factor = scale[e] * scale[e + lag] * live
            for m in range(2):
                value = looked(first + LOCAL + 2 * place + m) * factor
                obs[e, lag - 1, m] = value
                rhs[m, e] = rhs[m, e] - value
                rhs[m, e + lag] = rhs[m, e + lag] + value
    for copy in blocks + sides:
        copy.wait_send()

    for m in range(2):
        for j in range(BAND):
            p2_send[pl.ds(8 * (j // 4) + 4 * m + j % 4, ROWS, stride=WINDOW), :] = rhs[m, j]

    core = lax.rem(me, 2)
    chip = me // 2
    z, x = chip // 2, lax.rem(chip, 2)
    sibling = me + 1 - 2 * core
    planes = n_acq // 4
    half = ROWS // 2

    def place(zt, xt):
        both = lax.rem(zt, 2) == core
        return both | (xt == lax.rem(zt // 2 + core, 2)), 3 * (zt // 2) + jnp.where(both, xt, 2)

    def plane(turn):
        away = (planes - turn) // 2
        return rem(jnp.where(lax.rem(turn, 2) == 1, z + away, z - away), planes)

    to_sibling = pltpu.make_async_remote_copy(
        p2_send.at[pl.ds(pl.multiple_of((1 - core) * half * WINDOW, 8), half * WINDOW)],
        p2_sib, sib_ss, sib_rs, device_id=(sibling, col), device_id_type=MESH,
    )
    to_sibling.start()
    to_sibling.wait()
    mine_first = core == 0

    @pl.loop(0, half)
    def _(u):
        first, second = [], []
        for g in range(4):
            mine = p2_send[pl.ds(pl.multiple_of((core * half + u) * WINDOW + 8 * g, 8), 8), :]
            other = p2_sib[pl.ds(pl.multiple_of(u * WINDOW + 8 * g, 8), 8), :]
            first.append(jnp.where(mine_first, mine, other))
            second.append(jnp.where(mine_first, other, mine))
        total = [first[0]] + [first[g] + second[g - 1] for g in range(1, 4)] + [second[3]]
        p2_chip[pl.ds(pl.multiple_of(u * WIDE, 8), WIDE), :] = jnp.concatenate(total, axis=0)

    is_owner, row_me = place(z, x)

    @pl.loop(0, planes)
    def _(turn):
        zt = plane(turn)
        for xt in range(2):
            owns, u = place(zt, xt)
            target = 4 * zt + 2 * xt + core

            @pl.when(owns & (target != me))
            def _():
                pltpu.make_async_remote_copy(
                    p2_chip.at[pl.ds(pl.multiple_of(u * WIDE, 8), WIDE)],
                    p2_recv.at[pl.ds(pl.multiple_of(chip * WIDE, 8), WIDE)],
                    p2_ss, p2_rs, device_id=(target, col), device_id_type=MESH,
                ).start()

    def wait(ref, blocks, sem):
        part = ref.at[pl.ds(0, blocks * WIDE)]
        pltpu.make_async_copy(part, part, sem).wait()

    chips = n_acq // 2
    row_at = pl.multiple_of((core * half + row_me) * WIDE, 8)

    @pl.when(is_owner)
    def _():
        inverse[...] = ungrounded(eliminate(inverse[...], 16 - FIRST_GROUPS))
        p2_recv[pl.ds(pl.multiple_of(chip * WIDE, 8), WIDE), :] = p2_chip[
            pl.ds(pl.multiple_of(row_me * WIDE, 8), WIDE), :
        ]
        wait(p2_recv, chips - 1, p2_rs)
        groups = []
        for b in range(n_acq):
            total = None
            for g in range(b % 2, 5, 2):
                c = (b - g) // 2
                if c >= 0:
                    part = p2_recv[c * WIDE + 8 * g : c * WIDE + 8 * g + 8, :]
                    total = part if total is None else total + part
            groups.append(total)
        low = iota((8, COLS), 0) < 4
        first, second = [], []
        for v in range(n_acq // 2):
            one, two = groups[2 * v], groups[2 * v + 1]
            first.append(jnp.where(low, one, pltpu.roll(two, 4, axis=0)))
            second.append(jnp.where(low, pltpu.roll(one, 4, axis=0), two))
        sums = jnp.concatenate(
            [jnp.concatenate(first, axis=0), jnp.concatenate(second, axis=0)], axis=1
        )
        solved = jnp.dot(
            inverse[...], sums, precision=lax.Precision.HIGHEST, preferred_element_type=F32
        )
        for v in range(n_acq // 2):
            one, two = solved[8 * v : 8 * v + 8, :COLS], solved[8 * v : 8 * v + 8, COLS:]
            sol[16 * v : 16 * v + 8, :] = jnp.where(low, one, pltpu.roll(two, 4, axis=0))
            sol[16 * v + 8 : 16 * v + 16, :] = jnp.where(low, pltpu.roll(one, 4, axis=0), two)
        sol[8 * n_acq :, :] = jnp.zeros((24, COLS), F32)

        @pl.loop(0, planes)
        def _(turn):
            zt = turn
            for xt in range(2):
                target = 4 * zt + 2 * xt + core

                @pl.when(target != me)
                def _():
                    pltpu.make_async_remote_copy(
                        sol.at[pl.ds(pl.multiple_of((2 * zt + xt) * 16, 8), WIDE)],
                        p3_recv.at[pl.ds(row_at, WIDE)],
                        p3_ss, p3_rs, device_id=(target, col), device_id_type=MESH,
                    ).start()

        p3_recv[pl.ds(row_at, WIDE), :] = sol[pl.ds(pl.multiple_of(chip * 16, 8), WIDE), :]
        wait(p3_recv, half - 1, p3_rs)

    @pl.when(jnp.logical_not(is_owner))
    def _():
        wait(p3_recv, half, p3_rs)

    own_half = pl.ds(pl.multiple_of(core * half * WIDE, 8), half * WIDE)
    forward = pltpu.make_async_remote_copy(
        p3_recv.at[own_half], p3_recv.at[own_half], fw_ss, fw_rs,
        device_id=(sibling, col), device_id_type=MESH,
    )
    forward.start()

    @pl.when(is_owner)
    def _():
        wait(p2_chip, half - 1, p2_ss)
        wait(p2_recv, chips - 1, p3_ss)

    @pl.when(jnp.logical_not(is_owner))
    def _():
        wait(p2_chip, half, p2_ss)

    forward.wait()

    for m in range(2):
        for j in range(BAND):
            rhs[m, j] = p3_recv[pl.ds(8 * core + 8 * (j // 4) + 4 * m + j % 4, ROWS, stride=WIDE), :]
    for e in range(LOCAL):
        for m in range(2):
            disp_ref[e, m] = rhs[m, e]

    @pl.loop(0, LAGS)
    def _(k):
        for e in range(LOCAL):
            live = jnp.where(live_smem[k, LOCAL * me + e] > 0, 1.0, 0.0)
            for m in range(2):
                res_ref[e, k, m] = obs[e, k, m] - (rhs[m, e + k + 1] - rhs[m, e]) * live


def per_device(n_acq, n_col, samples, pair_live):
    vmem = pltpu.VMEM
    rows_all = BAND * ROWS + LAGS * LOCAL * GROUP
    return pl.pallas_call(
        functools.partial(kernel, n_acq, n_col),
        out_shape=(
            jax.ShapeDtypeStruct((LOCAL, 2, ROWS, COLS), F32),
            jax.ShapeDtypeStruct((LOCAL, LAGS, 2, ROWS, COLS), F32),
        ),
        in_specs=[
            pl.BlockSpec(memory_space=pltpu.HBM),
            pl.BlockSpec(memory_space=pltpu.HBM),
        ],
        out_specs=(pl.BlockSpec(memory_space=pltpu.VMEM), pl.BlockSpec(memory_space=pltpu.VMEM)),
        scratch_shapes=[
            vmem((BAND, 2, ROWS, COLS), F32),
            vmem((4, 2, ROWS, COLS), F32),
            vmem((2, ROWS, COLS), F32),
            vmem((rows_all, 2 * COLS), BF16),
            vmem((rows_all, 2 * COLS), BF16),
            vmem((2 * COLS, COLS), BF16),
            vmem((rows_all // ROWS, 40, COLS), F32),
            vmem((BAND, ROWS, COLS), F32),
            vmem((LOCAL, LAGS, 2, ROWS, COLS), F32),
            vmem((2, BAND, ROWS, COLS), F32),
            vmem((128, 128), F32),
            vmem((ROWS * WINDOW, COLS), F32),
            vmem((ROWS // 2 * WINDOW, COLS), F32),
            vmem((ROWS // 2 * WIDE, COLS), F32),
            vmem((n_acq // 2 * WIDE, COLS), F32),
            vmem((8 * n_acq + 24, COLS), F32),
            vmem((ROWS * WIDE, COLS), F32),
            vmem((LAGS, 4 * n_acq), jnp.int32),
            pltpu.SMEM((LAGS, 4 * n_acq), jnp.int32),
            pltpu.SemaphoreType.DMA,
            pltpu.SemaphoreType.DMA((2,)),
            pltpu.SemaphoreType.DMA((4,)),
            pltpu.SemaphoreType.DMA((4,)),
            pltpu.SemaphoreType.DMA((4, 2)),
            pltpu.SemaphoreType.DMA((4, 2)),
        ] + [pltpu.SemaphoreType.DMA] * 8,
        compiler_params=pltpu.CompilerParams(
            collective_id=0, has_side_effects=True, vmem_limit_bytes=32 * 1024 * 1024
        ),
    )(samples, pair_live.T)


def solution(mesh):
    return jax.shard_map(
        functools.partial(per_device, mesh.shape["acq"], mesh.shape["col"]),
        mesh=mesh,
        in_specs=(P("acq", None, None, "col"), P()),
        out_specs=(P("acq", None, None, "col"), P("acq", None, None, None, "col")),
        check_vma=False,
    )
```

```python
import functools

import jax
import jax.numpy as jnp
from jax import lax
from jax.experimental import pallas as pl
from jax.experimental.pallas import tpu as pltpu
from jax.sharding import PartitionSpec as P

MESH = pl.DeviceIdType.MESH
F32 = jnp.float32
BF16 = jnp.bfloat16
LOCAL = 4
PAIR = 8
CHAIN = 20
LAGS = 12
ROWS = 24
HALF = 12
PART = 16
COLS = 128
GROUP = 32
HALO = 10
WIDE = 40
FIRST_GROUPS = 5


def rem(a, n):
    return lax.rem(a + 4 * n, n)


def iota(shape, dim):
    return lax.broadcasted_iota(jnp.int32, shape, dim)


def split(value):
    high = value.astype(BF16)
    return high, (value - high.astype(F32)).astype(BF16)


def normal_matrix(live):
    n = live.shape[1]
    row, col = iota((n, n), 0), iota((n, n), 1)
    lower = jnp.zeros((n, n), F32)
    for k in range(LAGS):
        weight = jnp.where(live[k : k + 1, :] > 0, 1.0, 0.0)
        lower = lower + jnp.where(row == col + (k + 1), weight, 0.0)
    both = lower + lower.T
    degree = jnp.sum(both, axis=1, keepdims=True)
    full = jnp.where(row == col, degree, -both)
    grounded = jnp.where((row == 0) & (col == 0), 1.0, 0.0)
    return jnp.where((row == 0) | (col == 0), grounded, full)


def eliminate(matrix, groups):
    n = matrix.shape[0]
    lane, top = iota((1, n), 1), iota((8, n), 0)

    def group(_, a):
        for s in range(8):
            pivot = 1.0 / a[s : s + 1, s : s + 1]
            hit = lane == s
            scaled = jnp.where(hit, pivot, a[s : s + 1, :] * pivot)
            a = jnp.where(hit, 0.0, a) - a[:, s : s + 1] * scaled
            a = jnp.concatenate([jnp.where(top == s, scaled, a[:8]), a[8:]], axis=0)
        a = jnp.concatenate([a[8:], a[:8]], axis=0)
        return pltpu.roll(a, n - 8, axis=1)

    return lax.fori_loop(0, groups, group, matrix)


def ungrounded(inverse):
    row, col = iota(inverse.shape, 0), iota(inverse.shape, 1)
    return jnp.where((row == 0) | (col == 0), 0.0, inverse)


def box_weights():
    source, out = iota((COLS, COLS), 0), iota((COLS, COLS), 1)
    own = (source >= out - HALO) & (source < out + HALO)
    side = jnp.where(source >= 4 * HALO, source - 4 * HALO, source)
    for step in (2, 1):
        side = jnp.where(side >= step * HALO, side - step * HALO, side)
    left = (source < 4 * HALO) & (out <= side)
    right = (source >= 4 * HALO) & (source < 8 * HALO) & (out >= side + COLS - HALO + 1)
    return jnp.concatenate(
        [jnp.where(own, 1.0, 0.0), jnp.where(left | right, 1.0, 0.0)], axis=0
    ).astype(BF16)


def kernel(
    n_acq, n_col,
    x_ref, live_hbm, disp_ref, res_ref,
    main, edges, packed, lhs_hi, lhs_lo, weights, ypad, scale, obs, obs_in, rhs, disp,
    inverse, p2_chip, p2_recv, sol, p3_recv,
    live_ref, live_smem, live_sem, main_send, main_recv, edge_send, edge_recv,
    obs_ss, obs_rs, p2_ss, p2_rs, p3_ss, p3_rs, fw_ss, fw_rs,
):
    me, col = lax.axis_index("acq"), lax.axis_index("col")
    left, right = rem(col - 1, n_col), rem(col + 1, n_col)
    core, chip = lax.rem(me, 2), me // 2
    chips = n_acq // 2
    sibling = me + 1 - 2 * core
    lane = iota((ROWS, COLS), 1)

    lives = [
        pltpu.make_async_copy(live_hbm, live_ref, live_sem.at[0]),
        pltpu.make_async_copy(live_hbm, live_smem, live_sem.at[1]),
    ]
    for copy in lives:
        copy.start()

    barrier = pltpu.get_barrier_semaphore()

    def greet(target, where):
        pl.semaphore_signal(barrier, inc=1, device_id=(target, where), device_id_type=MESH)

    greet(sibling, col)

    @pl.loop(1, chips)
    def _(i):
        greet(2 * rem(chip + i, chips) + core, col)

    for i in (-2, -1, 1, 2):
        greet(2 * rem(chip + i, chips) + 1 - core, col)
    for side in (left, right):

        @pl.loop(-2, 3)
        def _(i):
            greet(2 * rem(chip + i, chips), side)
            greet(2 * rem(chip + i, chips) + 1, side)

    to_right = jnp.zeros((ROWS, COLS), F32)
    to_left = jnp.zeros((ROWS, COLS), F32)
    for m in range(2):
        for i in range(LOCAL):
            base = 4 * HALO * m + HALO * i
            hit = (lane >= base) & (lane < base + HALO)
            value = x_ref[i, m]
            to_right = jnp.where(hit, pltpu.roll(value, (base + HALO) % COLS, axis=1), to_right)
            to_left = jnp.where(hit, pltpu.roll(value, base, axis=1) if base else value, to_left)
    packed[0] = to_right
    packed[1] = to_left

    pl.semaphore_wait(barrier, chips + 4 + 20)

    def window(of_core):
        return pl.ds(pl.multiple_of(8 * of_core, 8), PART)

    def block(index):
        return main.at[pl.ds(LOCAL * index, LOCAL)]

    own = pltpu.make_async_copy(x_ref.at[:, :, window(core)], block(core), main_recv.at[core])
    own.start()
    sends, late_sends = [], []

    def send_block(number, target, of_core, index):
        return pltpu.make_async_remote_copy(
            x_ref.at[:, :, window(of_core)], block(index), main_send.at[number], main_recv.at[index],
            device_id=(target, col), device_id_type=MESH,
        )

    def send_edge(number, target, of_core, index, side):
        return pltpu.make_async_remote_copy(
            packed.at[side, window(of_core)], edges.at[index, side],
            edge_send.at[number, side], edge_recv.at[index, side],
            device_id=(target, (right, left)[side]), device_id_type=MESH,
        )

    for side in range(2):
        for to in range(2):
            sends.append(send_edge(to, 2 * chip + to, to, core, side))
    sends.append(send_block(0, sibling, 1 - core, core))
    earlier = 2 * rem(chip - 1, chips)
    for to in range(2):
        sends.append(send_block(1 + to, earlier + to, to, 2 + core))
    for to in range(2):
        for side in range(2):
            sends.append(send_edge(2 + to, earlier + to, to, 2 + core, side))
    earlier = 2 * rem(chip - 2, chips)
    for to in range(2):
        late_sends.append(send_block(3 + to, earlier + to, to, 4))
        for side in range(2):
            late_sends.append(send_edge(4 + to, earlier + to, to, 4, side))
    for copy in sends:
        copy.start()

    @pl.when(core == 0)
    def _():
        for copy in late_sends:
            copy.start()

    for copy in lives:
        copy.wait()
    inverse[...] = eliminate(normal_matrix(live_ref[...]), FIRST_GROUPS)
    weights[...] = box_weights()
    ypad[...] = jnp.zeros(ypad.shape, F32)
    rhs[...] = jnp.zeros(rhs.shape, F32)

    keep_left = jnp.where(col > 0, 1.0, 0.0)
    keep_right = jnp.where(col < n_col - 1, 1.0, 0.0)
    lane = iota((PART, COLS), 1)
    in_left = lane < 4 * HALO
    in_right = (lane >= 4 * HALO) & (lane < 8 * HALO)

    def slot_of(lanes, i):
        place = jnp.where(lanes >= 4 * HALO, lanes - 4 * HALO, lanes)
        return (place >= HALO * i) & (place < HALO * (i + 1)) & (lanes < 8 * HALO)

    lane_wide = iota((GROUP, COLS), 1)
    slots = [jnp.where(slot_of(lane_wide, i), 1.0, 0.0).astype(BF16) for i in range(LOCAL)]

    def turned(value, by):
        return pltpu.roll(value, by % COLS, axis=1) if by % COLS else value

    at_row = 0
    own_real, own_imag = [], []
    for b in range(5):
        pltpu.make_async_copy(block(b), block(b), main_recv.at[b]).wait()
        for side in range(2):
            pltpu.make_async_copy(edges.at[b, side], edges.at[b, side], edge_recv.at[b, side]).wait()
        low, high = edges[b, 0] * keep_left, edges[b, 1] * keep_right
        real = jnp.where(in_left, low, jnp.where(in_right, turned(high, 4 * HALO), 0.0))
        imag = jnp.where(in_left, turned(low, -4 * HALO), jnp.where(in_right, high, 0.0))
        if b < 2:
            own_real.append(real)
            own_imag.append(imag)
        first_row = at_row
        edge_power = real * real + imag * imag
        for h in range(2):
            parts, outer = [], []
            for i in (2 * h, 2 * h + 1):
                re, im = main[LOCAL * b + i, 0], main[LOCAL * b + i, 1]
                parts.append(re * re + im * im)
                outer.append(jnp.where(slot_of(lane, i), edge_power, 0.0))
            at = pl.ds(at_row, GROUP)
            lhs_hi[at, :COLS], lhs_lo[at, :COLS] = split(jnp.concatenate(parts, axis=0))
            lhs_hi[at, COLS:], lhs_lo[at, COLS:] = split(jnp.concatenate(outer, axis=0))
            at_row += GROUP
        pairs = []
        for q, t in [(q, t) for q in range(min(b + 1, 2)) for t in range(-3, 4)]:
            lag = 4 * (b - q) + t
            if not 1 <= lag <= LAGS:
                continue
            later_re, later_im = turned(real, -HALO * t), turned(imag, -HALO * t)
            side_hi, side_lo = split(
                jnp.concatenate(
                    [
                        own_real[q] * later_re + own_imag[q] * later_im,
                        own_imag[q] * later_re - own_real[q] * later_im,
                    ],
                    axis=0,
                )
            )
            for i in range(max(0, -t), min(LOCAL, LOCAL - t)):
                e = LOCAL * q + i
                re, im = main[e, 0], main[e, 1]
                re_j, im_j = main[e + lag, 0], main[e + lag, 1]
                cross = jnp.concatenate([re * re_j + im * im_j, im * re_j - re * im_j], axis=0)
                at = pl.ds(at_row, GROUP)
                lhs_hi[at, :COLS], lhs_lo[at, :COLS] = split(cross)
                lhs_hi[at, COLS:] = side_hi * slots[i]
                lhs_lo[at, COLS:] = side_lo * slots[i]
                at_row += GROUP
                pairs.append((e, lag))

        at = pl.ds(first_row, at_row - first_row)
        by_cols = jnp.dot(lhs_hi[at, :], weights[...], preferred_element_type=F32)
        by_cols = by_cols + jnp.dot(lhs_lo[at, :], weights[...], preferred_element_type=F32)
        first, count = first_row // PART, (at_row - first_row) // PART
        ypad[pl.ds(first, count), 8 : 8 + PART, :] = by_cols.reshape(count, PART, COLS)

        def looked(i):
            total = ypad[i, 6 : 6 + PART, :]
            for step in range(1, 5):
                total = total + ypad[i, 6 + step : 6 + step + PART, :]
            return total

        for i in range(LOCAL):
            scale[LOCAL * b + i] = lax.rsqrt(looked(first + i))
        for place, (e, lag) in enumerate(pairs):
            live = jnp.where(live_smem[lag - 1, PAIR * chip + e] > 0, 1.0, 0.0)
            factor = scale[e] * scale[e + lag] * live
            for m in range(2):
                value = looked(first + LOCAL + 2 * place + m) * factor
                obs[e // LOCAL, e % LOCAL, lag - 1, m] = value
                rhs[m, e] = rhs[m, e] - value
                rhs[m, e + lag] = rhs[m, e + lag] + value

    for m in range(2):
        for j in range(CHAIN):
            p2_chip[pl.ds(8 * (j // 4) + 4 * m + j % 4, PART, stride=WIDE), :] = rhs[m, j]

    z, x = chip // 2, lax.rem(chip, 2)
    planes = n_acq // 4
    half = HALF
    skip = 4 * core

    def place(zt, xt):
        both = lax.rem(zt, 2) == core
        return both | (xt == lax.rem(zt // 2 + core, 2)), 3 * (zt // 2) + jnp.where(both, xt, 2)

    def plane(turn):
        away = (planes - turn) // 2
        return rem(jnp.where(lax.rem(turn, 2) == 1, z + away, z - away), planes)

    is_owner, row_me = place(z, x)

    @pl.loop(0, planes)
    def _(turn):
        zt = plane(turn)
        for xt in range(2):
            owns, u = place(zt, xt)
            target = 4 * zt + 2 * xt + core

            @pl.when(owns & (target != me))
            def _():
                pltpu.make_async_remote_copy(
                    p2_chip.at[pl.ds(pl.multiple_of((u + skip) * WIDE, 8), WIDE)],
                    p2_recv.at[pl.ds(pl.multiple_of(chip * WIDE, 8), WIDE)],
                    p2_ss, p2_rs, device_id=(target, col), device_id_type=MESH,
                ).start()

    to_sibling = pltpu.make_async_remote_copy(
        obs.at[1 - core], obs_in, obs_ss, obs_rs, device_id=(sibling, col), device_id_type=MESH
    )
    to_sibling.start()

    def wait(ref, blocks, sem):
        part = ref.at[pl.ds(0, blocks * WIDE)]
        pltpu.make_async_copy(part, part, sem).wait()

    row_at = pl.multiple_of((core * half + row_me) * WIDE, 8)

    @pl.when(is_owner)
    def _():
        inverse[...] = ungrounded(eliminate(inverse[...], 16 - FIRST_GROUPS))
        p2_recv[pl.ds(pl.multiple_of(chip * WIDE, 8), WIDE), :] = p2_chip[
            pl.ds(pl.multiple_of((row_me + skip) * WIDE, 8), WIDE), :
        ]
        wait(p2_recv, chips - 1, p2_rs)
        groups = []
        for b in range(n_acq):
            total = None
            for g in range(b % 2, 5, 2):
                c = (b - g) // 2
                if c >= 0:
                    part = p2_recv[c * WIDE + 8 * g : c * WIDE + 8 * g + 8, :]
                    total = part if total is None else total + part
            groups.append(total)
        low = iota((8, COLS), 0) < 4
        first, second = [], []
        for v in range(n_acq // 2):
            one, two = groups[2 * v], groups[2 * v + 1]
            first.append(jnp.where(low, one, pltpu.roll(two, 4, axis=0)))
            second.append(jnp.where(low, pltpu.roll(one, 4, axis=0), two))
        sums = jnp.concatenate(
            [jnp.concatenate(first, axis=0), jnp.concatenate(second, axis=0)], axis=1
        )
        solved = jnp.dot(
            inverse[...], sums, precision=lax.Precision.HIGHEST, preferred_element_type=F32
        )
        for v in range(n_acq // 2):
            one, two = solved[8 * v : 8 * v + 8, :COLS], solved[8 * v : 8 * v + 8, COLS:]
            sol[16 * v : 16 * v + 8, :] = jnp.where(low, one, pltpu.roll(two, 4, axis=0))
            sol[16 * v + 8 : 16 * v + 16, :] = jnp.where(low, pltpu.roll(one, 4, axis=0), two)
        sol[8 * n_acq :, :] = jnp.zeros((24, COLS), F32)

        @pl.loop(0, planes)
        def _(turn):
            zt = turn
            for xt in range(2):
                target = 4 * zt + 2 * xt + core

                @pl.when(target != me)
                def _():
                    pltpu.make_async_remote_copy(
                        sol.at[pl.ds(pl.multiple_of((2 * zt + xt) * 16, 8), WIDE)],
                        p3_recv.at[pl.ds(row_at, WIDE)],
                        p3_ss, p3_rs, device_id=(target, col), device_id_type=MESH,
                    ).start()

        p3_recv[pl.ds(row_at, WIDE), :] = sol[pl.ds(pl.multiple_of(chip * 16, 8), WIDE), :]
        wait(p3_recv, half - 1, p3_rs)

    @pl.when(jnp.logical_not(is_owner))
    def _():
        wait(p3_recv, half, p3_rs)

    own_half = pl.ds(pl.multiple_of(core * half * WIDE, 8), half * WIDE)
    forward = pltpu.make_async_remote_copy(
        p3_recv.at[own_half], p3_recv.at[own_half], fw_ss, fw_rs,
        device_id=(sibling, col), device_id_type=MESH,
    )
    forward.start()

    @pl.when(is_owner)
    def _():
        wait(p2_chip, half - 1, p2_ss)
        wait(p2_recv, chips - 1, p3_ss)

    @pl.when(jnp.logical_not(is_owner))
    def _():
        wait(p2_chip, half, p2_ss)

    for copy in sends:
        copy.wait_send()

    @pl.when(core == 0)
    def _():
        for copy in late_sends:
            copy.wait_send()

    to_sibling.wait()
    forward.wait()

    for m in range(2):
        for j in range(16):
            disp[m, j] = p3_recv[pl.ds(8 * core + 8 * (j // 4) + 4 * m + j % 4, ROWS, stride=WIDE), :]
    for e in range(LOCAL):
        for m in range(2):
            disp_ref[e, m] = disp[m, e]
    upper = iota((8, COLS), 0) < 4
    on_first = core == 0

    @pl.loop(0, LAGS)
    def _(k):
        for e in range(LOCAL):
            live = jnp.where(live_smem[k, LOCAL * me + e] > 0, 1.0, 0.0)
            for m in range(2):
                mine, other = obs[core, e, k, m], obs_in[e, k, m]
                low, high = jnp.where(on_first, mine, other), jnp.where(on_first, other, mine)
                seen = jnp.concatenate(
                    [low[:8], jnp.where(upper, low[8:], high[:8]), high[8:]], axis=0
                )
                res_ref[e, k, m] = seen - (disp[m, e + k + 1] - disp[m, e]) * live


def per_device(n_acq, n_col, samples, pair_live):
    vmem = pltpu.VMEM
    rows_all = CHAIN * PART + LAGS * PAIR * GROUP
    return pl.pallas_call(
        functools.partial(kernel, n_acq, n_col),
        out_shape=(
            jax.ShapeDtypeStruct((LOCAL, 2, ROWS, COLS), F32),
            jax.ShapeDtypeStruct((LOCAL, LAGS, 2, ROWS, COLS), F32),
        ),
        in_specs=[
            pl.BlockSpec(memory_space=pltpu.VMEM),
            pl.BlockSpec(memory_space=pltpu.HBM),
        ],
        out_specs=(pl.BlockSpec(memory_space=pltpu.VMEM), pl.BlockSpec(memory_space=pltpu.VMEM)),
        scratch_shapes=[
            vmem((CHAIN, 2, PART, COLS), F32),
            vmem((5, 2, PART, COLS), F32),
            vmem((2, ROWS, COLS), F32),
            vmem((rows_all, 2 * COLS), BF16),
            vmem((rows_all, 2 * COLS), BF16),
            vmem((2 * COLS, COLS), BF16),
            vmem((rows_all // PART, 32, COLS), F32),
            vmem((CHAIN, PART, COLS), F32),
            vmem((2, LOCAL, LAGS, 2, PART, COLS), F32),
            vmem((LOCAL, LAGS, 2, PART, COLS), F32),
            vmem((2, CHAIN, PART, COLS), F32),
            vmem((2, 16, ROWS, COLS), F32),
            vmem((128, 128), F32),
            vmem((PART * WIDE, COLS), F32),
            vmem((n_acq // 2 * WIDE, COLS), F32),
            vmem((8 * n_acq + 24, COLS), F32),
            vmem((ROWS * WIDE, COLS), F32),
            vmem((LAGS, 4 * n_acq), jnp.int32),
            pltpu.SMEM((LAGS, 4 * n_acq), jnp.int32),
            pltpu.SemaphoreType.DMA((2,)),
            pltpu.SemaphoreType.DMA((5,)),
            pltpu.SemaphoreType.DMA((5,)),
            pltpu.SemaphoreType.DMA((6, 2)),
            pltpu.SemaphoreType.DMA((5, 2)),
        ] + [pltpu.SemaphoreType.DMA] * 8,
        compiler_params=pltpu.CompilerParams(
            collective_id=0, has_side_effects=True, vmem_limit_bytes=32 * 1024 * 1024
        ),
    )(samples, pair_live.T)


def solution(mesh):
    return jax.shard_map(
        functools.partial(per_device, mesh.shape["acq"], mesh.shape["col"]),
        mesh=mesh,
        in_specs=(P("acq", None, None, "col"), P()),
        out_specs=(P("acq", None, None, "col"), P("acq", None, None, None, "col")),
        check_vma=False,
    )
```

```python
import functools

import jax
import jax.numpy as jnp
from jax import lax
from jax.experimental import pallas as pl
from jax.experimental.pallas import tpu as pltpu
from jax.sharding import PartitionSpec as P

MESH = pl.DeviceIdType.MESH
F32 = jnp.float32
BF16 = jnp.bfloat16
LOCAL = 4
PAIR = 8
CHAIN = 20
LAGS = 12
ROWS = 24
HALF = 12
PART = 16
COLS = 128
GROUP = 32
HALO = 10
WIDE = 40
FIRST_GROUPS = 5


def rem(a, n):
    return lax.rem(a + 4 * n, n)


def iota(shape, dim):
    return lax.broadcasted_iota(jnp.int32, shape, dim)


def split(value):
    high = value.astype(BF16)
    return high, (value - high.astype(F32)).astype(BF16)


def normal_matrix(live):
    n = live.shape[1]
    row, col = iota((n, n), 0), iota((n, n), 1)
    lower = jnp.zeros((n, n), F32)
    for k in range(LAGS):
        weight = jnp.where(live[k : k + 1, :] > 0, 1.0, 0.0)
        lower = lower + jnp.where(row == col + (k + 1), weight, 0.0)
    both = lower + lower.T
    degree = jnp.sum(both, axis=1, keepdims=True)
    full = jnp.where(row == col, degree, -both)
    grounded = jnp.where((row == 0) & (col == 0), 1.0, 0.0)
    return jnp.where((row == 0) | (col == 0), grounded, full)


def eliminate(matrix, groups):
    n = matrix.shape[0]
    lane, top = iota((1, n), 1), iota((8, n), 0)

    def group(_, a):
        for s in range(8):
            pivot = 1.0 / a[s : s + 1, s : s + 1]
            hit = lane == s
            scaled = jnp.where(hit, pivot, a[s : s + 1, :] * pivot)
            a = jnp.where(hit, 0.0, a) - a[:, s : s + 1] * scaled
            a = jnp.concatenate([jnp.where(top == s, scaled, a[:8]), a[8:]], axis=0)
        a = jnp.concatenate([a[8:], a[:8]], axis=0)
        return pltpu.roll(a, n - 8, axis=1)

    return lax.fori_loop(0, groups, group, matrix)


def ungrounded(inverse):
    row, col = iota(inverse.shape, 0), iota(inverse.shape, 1)
    return jnp.where((row == 0) | (col == 0), 0.0, inverse)


def box_weights():
    source, out = iota((COLS, COLS), 0), iota((COLS, COLS), 1)
    own = (source >= out - HALO) & (source < out + HALO)
    side = jnp.where(source >= 4 * HALO, source - 4 * HALO, source)
    for step in (2, 1):
        side = jnp.where(side >= step * HALO, side - step * HALO, side)
    left = (source < 4 * HALO) & (out <= side)
    right = (source >= 4 * HALO) & (source < 8 * HALO) & (out >= side + COLS - HALO + 1)
    return jnp.concatenate(
        [jnp.where(own, 1.0, 0.0), jnp.where(left | right, 1.0, 0.0)], axis=0
    ).astype(BF16)


def kernel(
    n_acq, n_col,
    x_hbm, live_hbm, disp_ref, res_ref,
    main, edges, packed, lhs_hi, lhs_lo, weights, ypad, scale, obs, obs_in, rhs, disp,
    inverse, p2_chip, p2_recv, sol, p3_recv,
    x_ref, live_ref, live_smem, own_sem, live_sem, main_send, main_recv, edge_send, edge_recv,
    obs_ss, obs_rs, p2_ss, p2_rs, p3_ss, p3_rs, fw_ss, fw_rs,
):
    me, col = lax.axis_index("acq"), lax.axis_index("col")
    left, right = rem(col - 1, n_col), rem(col + 1, n_col)
    core, chip = lax.rem(me, 2), me // 2
    chips = n_acq // 2
    sibling = me + 1 - 2 * core
    lane = iota((ROWS, COLS), 1)

    fetch = pltpu.make_async_copy(x_hbm, x_ref, own_sem)
    fetch.start()
    lives = [
        pltpu.make_async_copy(live_hbm, live_ref, live_sem.at[0]),
        pltpu.make_async_copy(live_hbm, live_smem, live_sem.at[1]),
    ]
    for copy in lives:
        copy.start()

    barrier = pltpu.get_barrier_semaphore()

    def greet(target, where):
        pl.semaphore_signal(barrier, inc=1, device_id=(target, where), device_id_type=MESH)

    greet(sibling, col)

    @pl.loop(1, chips)
    def _(i):
        greet(2 * rem(chip + i, chips) + core, col)

    for i in (-2, -1, 1, 2):
        greet(2 * rem(chip + i, chips) + 1 - core, col)
    for side in (left, right):

        @pl.loop(-2, 3)
        def _(i):
            greet(2 * rem(chip + i, chips), side)
            greet(2 * rem(chip + i, chips) + 1, side)

    fetch.wait()
    to_right = jnp.zeros((ROWS, COLS), F32)
    to_left = jnp.zeros((ROWS, COLS), F32)
    for m in range(2):
        for i in range(LOCAL):
            base = 4 * HALO * m + HALO * i
            hit = (lane >= base) & (lane < base + HALO)
            value = x_ref[i, m]
            to_right = jnp.where(hit, pltpu.roll(value, (base + HALO) % COLS, axis=1), to_right)
            to_left = jnp.where(hit, pltpu.roll(value, base, axis=1) if base else value, to_left)
    packed[0] = to_right
    packed[1] = to_left

    pl.semaphore_wait(barrier, chips + 4 + 20)

    def window(of_core):
        return pl.ds(pl.multiple_of(8 * of_core, 8), PART)

    def block(index):
        return main.at[pl.ds(LOCAL * index, LOCAL)]

    own = pltpu.make_async_copy(x_ref.at[:, :, window(core)], block(core), main_recv.at[core])
    own.start()
    sends, late_sends = [], []

    def send_block(number, target, of_core, index):
        return pltpu.make_async_remote_copy(
            x_ref.at[:, :, window(of_core)], block(index), main_send.at[number], main_recv.at[index],
            device_id=(target, col), device_id_type=MESH,
        )

    def send_edge(number, target, of_core, index, side):
        return pltpu.make_async_remote_copy(
            packed.at[side, window(of_core)], edges.at[index, side],
            edge_send.at[number, side], edge_recv.at[index, side],
            device_id=(target, (right, left)[side]), device_id_type=MESH,
        )

    for side in range(2):
        for to in range(2):
            sends.append(send_edge(to, 2 * chip + to, to, core, side))
    sends.append(send_block(0, sibling, 1 - core, core))
    earlier = 2 * rem(chip - 1, chips)
    for to in range(2):
        sends.append(send_block(1 + to, earlier + to, to, 2 + core))
    for to in range(2):
        for side in range(2):
            sends.append(send_edge(2 + to, earlier + to, to, 2 + core, side))
    earlier = 2 * rem(chip - 2, chips)
    for to in range(2):
        late_sends.append(send_block(3 + to, earlier + to, to, 4))
        for side in range(2):
            late_sends.append(send_edge(4 + to, earlier + to, to, 4, side))
    for copy in sends:
        copy.start()

    @pl.when(core == 0)
    def _():
        for copy in late_sends:
            copy.start()

    for copy in lives:
        copy.wait()
    inverse[...] = eliminate(normal_matrix(live_ref[...]), FIRST_GROUPS)
    weights[...] = box_weights()
    ypad[...] = jnp.zeros(ypad.shape, F32)
    rhs[...] = jnp.zeros(rhs.shape, F32)

    keep_left = jnp.where(col > 0, 1.0, 0.0)
    keep_right = jnp.where(col < n_col - 1, 1.0, 0.0)
    lane = iota((PART, COLS), 1)
    in_left = lane < 4 * HALO
    in_right = (lane >= 4 * HALO) & (lane < 8 * HALO)

    def slot_of(lanes, i):
        place = jnp.where(lanes >= 4 * HALO, lanes - 4 * HALO, lanes)
        return (place >= HALO * i) & (place < HALO * (i + 1)) & (lanes < 8 * HALO)

    lane_wide = iota((GROUP, COLS), 1)
    slots = [jnp.where(slot_of(lane_wide, i), 1.0, 0.0).astype(BF16) for i in range(LOCAL)]

    def turned(value, by):
        return pltpu.roll(value, by % COLS, axis=1) if by % COLS else value

    at_row = 0
    own_real, own_imag = [], []
    for b in range(5):
        pltpu.make_async_copy(block(b), block(b), main_recv.at[b]).wait()
        for side in range(2):
            pltpu.make_async_copy(edges.at[b, side], edges.at[b, side], edge_recv.at[b, side]).wait()
        low, high = edges[b, 0] * keep_left, edges[b, 1] * keep_right
        real = jnp.where(in_left, low, jnp.where(in_right, turned(high, 4 * HALO), 0.0))
        imag = jnp.where(in_left, turned(low, -4 * HALO), jnp.where(in_right, high, 0.0))
        if b < 2:
            own_real.append(real)
            own_imag.append(imag)
        first_row = at_row
        edge_power = real * real + imag * imag
        for h in range(2):
            parts, outer = [], []
            for i in (2 * h, 2 * h + 1):
                re, im = main[LOCAL * b + i, 0], main[LOCAL * b + i, 1]
                parts.append(re * re + im * im)
                outer.append(jnp.where(slot_of(lane, i), edge_power, 0.0))
            at = pl.ds(at_row, GROUP)
            lhs_hi[at, :COLS], lhs_lo[at, :COLS] = split(jnp.concatenate(parts, axis=0))
            lhs_hi[at, COLS:], lhs_lo[at, COLS:] = split(jnp.concatenate(outer, axis=0))
            at_row += GROUP
        pairs = []
        for q, t in [(q, t) for q in range(min(b + 1, 2)) for t in range(-3, 4)]:
            lag = 4 * (b - q) + t
            if not 1 <= lag <= LAGS:
                continue
            later_re, later_im = turned(real, -HALO * t), turned(imag, -HALO * t)
            side_hi, side_lo = split(
                jnp.concatenate(
                    [
                        own_real[q] * later_re + own_imag[q] * later_im,
                        own_imag[q] * later_re - own_real[q] * later_im,
                    ],
                    axis=0,
                )
            )
            for i in range(max(0, -t), min(LOCAL, LOCAL - t)):
                e = LOCAL * q + i
                re, im = main[e, 0], main[e, 1]
                re_j, im_j = main[e + lag, 0], main[e + lag, 1]
                cross = jnp.concatenate([re * re_j + im * im_j, im * re_j - re * im_j], axis=0)
                at = pl.ds(at_row, GROUP)
                lhs_hi[at, :COLS], lhs_lo[at, :COLS] = split(cross)
                lhs_hi[at, COLS:] = side_hi * slots[i]
                lhs_lo[at, COLS:] = side_lo * slots[i]
                at_row += GROUP
                pairs.append((e, lag))

        at = pl.ds(first_row, at_row - first_row)
        by_cols = jnp.dot(lhs_hi[at, :], weights[...], preferred_element_type=F32)
        by_cols = by_cols + jnp.dot(lhs_lo[at, :], weights[...], preferred_element_type=F32)
        first, count = first_row // PART, (at_row - first_row) // PART
        ypad[pl.ds(first, count), 8 : 8 + PART, :] = by_cols.reshape(count, PART, COLS)

        def looked(i):
            total = ypad[i, 6 : 6 + PART, :]
            for step in range(1, 5):
                total = total + ypad[i, 6 + step : 6 + step + PART, :]
            return total

        for i in range(LOCAL):
            scale[LOCAL * b + i] = lax.rsqrt(looked(first + i))
        for place, (e, lag) in enumerate(pairs):
            live = jnp.where(live_smem[lag - 1, PAIR * chip + e] > 0, 1.0, 0.0)
            factor = scale[e] * scale[e + lag] * live
            for m in range(2):
                value = looked(first + LOCAL + 2 * place + m) * factor
                obs[e // LOCAL, e % LOCAL, lag - 1, m] = value
                rhs[m, e] = rhs[m, e] - value
                rhs[m, e + lag] = rhs[m, e + lag] + value

    for m in range(2):
        for j in range(CHAIN):
            p2_chip[pl.ds(8 * (j // 4) + 4 * m + j % 4, PART, stride=WIDE), :] = rhs[m, j]

    z, x = chip // 2, lax.rem(chip, 2)
    planes = n_acq // 4
    half = HALF
    skip = 4 * core

    def place(zt, xt):
        both = lax.rem(zt, 2) == core
        return both | (xt == lax.rem(zt // 2 + core, 2)), 3 * (zt // 2) + jnp.where(both, xt, 2)

    def plane(turn):
        away = (planes - turn) // 2
        return rem(jnp.where(lax.rem(turn, 2) == 1, z + away, z - away), planes)

    is_owner, row_me = place(z, x)

    @pl.loop(0, planes)
    def _(turn):
        zt = plane(turn)
        for xt in range(2):
            owns, u = place(zt, xt)
            target = 4 * zt + 2 * xt + core

            @pl.when(owns & (target != me))
            def _():
                pltpu.make_async_remote_copy(
                    p2_chip.at[pl.ds(pl.multiple_of((u + skip) * WIDE, 8), WIDE)],
                    p2_recv.at[pl.ds(pl.multiple_of(chip * WIDE, 8), WIDE)],
                    p2_ss, p2_rs, device_id=(target, col), device_id_type=MESH,
                ).start()

    to_sibling = pltpu.make_async_remote_copy(
        obs.at[1 - core], obs_in, obs_ss, obs_rs, device_id=(sibling, col), device_id_type=MESH
    )
    to_sibling.start()

    def wait(ref, blocks, sem):
        part = ref.at[pl.ds(0, blocks * WIDE)]
        pltpu.make_async_copy(part, part, sem).wait()

    row_at = pl.multiple_of((core * half + row_me) * WIDE, 8)

    @pl.when(is_owner)
    def _():
        inverse[...] = ungrounded(eliminate(inverse[...], 16 - FIRST_GROUPS))
        p2_recv[pl.ds(pl.multiple_of(chip * WIDE, 8), WIDE), :] = p2_chip[
            pl.ds(pl.multiple_of((row_me + skip) * WIDE, 8), WIDE), :
        ]
        wait(p2_recv, chips - 1, p2_rs)
        groups = []
        for b in range(n_acq):
            total = None
            for g in range(b % 2, 5, 2):
                c = (b - g) // 2
                if c >= 0:
                    part = p2_recv[c * WIDE + 8 * g : c * WIDE + 8 * g + 8, :]
                    total = part if total is None else total + part
            groups.append(total)
        low = iota((8, COLS), 0) < 4
        first, second = [], []
        for v in range(n_acq // 2):
            one, two = groups[2 * v], groups[2 * v + 1]
            first.append(jnp.where(low, one, pltpu.roll(two, 4, axis=0)))
            second.append(jnp.where(low, pltpu.roll(one, 4, axis=0), two))
        sums = jnp.concatenate(
            [jnp.concatenate(first, axis=0), jnp.concatenate(second, axis=0)], axis=1
        )
        solved = jnp.dot(
            inverse[...], sums, precision=lax.Precision.HIGHEST, preferred_element_type=F32
        )
        for v in range(n_acq // 2):
            one, two = solved[8 * v : 8 * v + 8, :COLS], solved[8 * v : 8 * v + 8, COLS:]
            sol[16 * v : 16 * v + 8, :] = jnp.where(low, one, pltpu.roll(two, 4, axis=0))
            sol[16 * v + 8 : 16 * v + 16, :] = jnp.where(low, pltpu.roll(one, 4, axis=0), two)
        sol[8 * n_acq :, :] = jnp.zeros((24, COLS), F32)

        @pl.loop(0, planes)
        def _(turn):
            zt = turn
            for xt in range(2):
                target = 4 * zt + 2 * xt + core

                @pl.when(target != me)
                def _():
                    pltpu.make_async_remote_copy(
                        sol.at[pl.ds(pl.multiple_of((2 * zt + xt) * 16, 8), WIDE)],
                        p3_recv.at[pl.ds(row_at, WIDE)],
                        p3_ss, p3_rs, device_id=(target, col), device_id_type=MESH,
                    ).start()

        p3_recv[pl.ds(row_at, WIDE), :] = sol[pl.ds(pl.multiple_of(chip * 16, 8), WIDE), :]
        wait(p3_recv, half - 1, p3_rs)

    @pl.when(jnp.logical_not(is_owner))
    def _():
        wait(p3_recv, half, p3_rs)

    own_half = pl.ds(pl.multiple_of(core * half * WIDE, 8), half * WIDE)
    forward = pltpu.make_async_remote_copy(
        p3_recv.at[own_half], p3_recv.at[own_half], fw_ss, fw_rs,
        device_id=(sibling, col), device_id_type=MESH,
    )
    forward.start()

    @pl.when(is_owner)
    def _():
        wait(p2_chip, half - 1, p2_ss)
        wait(p2_recv, chips - 1, p3_ss)

    @pl.when(jnp.logical_not(is_owner))
    def _():
        wait(p2_chip, half, p2_ss)

    for copy in sends:
        copy.wait_send()

    @pl.when(core == 0)
    def _():
        for copy in late_sends:
            copy.wait_send()

    to_sibling.wait()
    forward.wait()

    for m in range(2):
        for j in range(16):
            disp[m, j] = p3_recv[pl.ds(8 * core + 8 * (j // 4) + 4 * m + j % 4, ROWS, stride=WIDE), :]
    for e in range(LOCAL):
        for m in range(2):
            disp_ref[e, m] = disp[m, e]
    upper = iota((8, COLS), 0) < 4
    on_first = core == 0

    @pl.loop(0, LAGS)
    def _(k):
        for e in range(LOCAL):
            live = jnp.where(live_smem[k, LOCAL * me + e] > 0, 1.0, 0.0)
            for m in range(2):
                mine, other = obs[core, e, k, m], obs_in[e, k, m]
                low, high = jnp.where(on_first, mine, other), jnp.where(on_first, other, mine)
                seen = jnp.concatenate(
                    [low[:8], jnp.where(upper, low[8:], high[:8]), high[8:]], axis=0
                )
                res_ref[e, k, m] = seen - (disp[m, e + k + 1] - disp[m, e]) * live


def place_out(disp_in, res_in, disp_out, res_out, sems):
    copies = [pltpu.make_async_copy(disp_in, disp_out, sems.at[LOCAL])]
    for e in range(LOCAL):
        copies.append(pltpu.make_async_copy(res_in.at[e], res_out.at[e], sems.at[e]))
    for copy in copies:
        copy.start()
    for copy in copies:
        copy.wait()


def per_device(n_acq, n_col, samples, pair_live):
    vmem = pltpu.VMEM
    rows_all = CHAIN * PART + LAGS * PAIR * GROUP
    results = pl.pallas_call(
        functools.partial(kernel, n_acq, n_col),
        out_shape=(
            jax.ShapeDtypeStruct((LOCAL, 2, ROWS, COLS), F32),
            jax.ShapeDtypeStruct((LOCAL, LAGS, 2, ROWS, COLS), F32),
        ),
        in_specs=[
            pl.BlockSpec(memory_space=pltpu.HBM),
            pl.BlockSpec(memory_space=pltpu.HBM),
        ],
        out_specs=(pl.BlockSpec(memory_space=pltpu.VMEM), pl.BlockSpec(memory_space=pltpu.VMEM)),
        scratch_shapes=[
            vmem((CHAIN, 2, PART, COLS), F32),
            vmem((5, 2, PART, COLS), F32),
            vmem((2, ROWS, COLS), F32),
            vmem((rows_all, 2 * COLS), BF16),
            vmem((rows_all, 2 * COLS), BF16),
            vmem((2 * COLS, COLS), BF16),
            vmem((rows_all // PART, 32, COLS), F32),
            vmem((CHAIN, PART, COLS), F32),
            vmem((2, LOCAL, LAGS, 2, PART, COLS), F32),
            vmem((LOCAL, LAGS, 2, PART, COLS), F32),
            vmem((2, CHAIN, PART, COLS), F32),
            vmem((2, 16, ROWS, COLS), F32),
            vmem((128, 128), F32),
            vmem((PART * WIDE, COLS), F32),
            vmem((n_acq // 2 * WIDE, COLS), F32),
            vmem((8 * n_acq + 24, COLS), F32),
            vmem((ROWS * WIDE, COLS), F32),
            vmem((LOCAL, 2, ROWS, COLS), F32),
            vmem((LAGS, 4 * n_acq), jnp.int32),
            pltpu.SMEM((LAGS, 4 * n_acq), jnp.int32),
            pltpu.SemaphoreType.DMA,
            pltpu.SemaphoreType.DMA((2,)),
            pltpu.SemaphoreType.DMA((5,)),
            pltpu.SemaphoreType.DMA((5,)),
            pltpu.SemaphoreType.DMA((6, 2)),
            pltpu.SemaphoreType.DMA((5, 2)),
        ] + [pltpu.SemaphoreType.DMA] * 8,
        compiler_params=pltpu.CompilerParams(
            collective_id=0, has_side_effects=True, vmem_limit_bytes=32 * 1024 * 1024
        ),
    )(pltpu.with_memory_space_constraint(samples, pltpu.HBM), pltpu.with_memory_space_constraint(pair_live.T, pltpu.HBM))
    return pl.pallas_call(
        place_out,
        out_shape=tuple(jax.ShapeDtypeStruct(r.shape, F32) for r in results),
        in_specs=[pl.BlockSpec(memory_space=pl.ANY)] * 2,
        out_specs=(pl.BlockSpec(memory_space=pl.ANY),) * 2,
        scratch_shapes=[pltpu.SemaphoreType.DMA((LOCAL + 1,))],
        compiler_params=pltpu.CompilerParams(vmem_limit_bytes=4 * 1024 * 1024),
    )(*results)


def solution(mesh):
    return jax.shard_map(
        functools.partial(per_device, mesh.shape["acq"], mesh.shape["col"]),
        mesh=mesh,
        in_specs=(P("acq", None, None, "col"), P()),
        out_specs=(P("acq", None, None, "col"), P("acq", None, None, None, "col")),
        check_vma=False,
    )
```

```python
import functools

import jax
import jax.numpy as jnp
from jax import lax
from jax.experimental import pallas as pl
from jax.experimental.pallas import tpu as pltpu
from jax.sharding import PartitionSpec as P

MESH = pl.DeviceIdType.MESH
F32 = jnp.float32
BF16 = jnp.bfloat16
LOCAL = 4
PAIR = 8
CHAIN = 20
LAGS = 12
ROWS = 24
HALF = 12
PART = 16
COLS = 128
GROUP = 32
HALO = 10
WIDE = 40
FIRST_GROUPS = 5


def rem(a, n):
    return lax.rem(a + 4 * n, n)


def iota(shape, dim):
    return lax.broadcasted_iota(jnp.int32, shape, dim)


def split(value):
    high = value.astype(BF16)
    return high, (value - high.astype(F32)).astype(BF16)


def normal_matrix(live):
    n = live.shape[1]
    row, col = iota((n, n), 0), iota((n, n), 1)
    lower = jnp.zeros((n, n), F32)
    for k in range(LAGS):
        weight = jnp.where(live[k : k + 1, :] > 0, 1.0, 0.0)
        lower = lower + jnp.where(row == col + (k + 1), weight, 0.0)
    both = lower + lower.T
    degree = jnp.sum(both, axis=1, keepdims=True)
    full = jnp.where(row == col, degree, -both)
    grounded = jnp.where((row == 0) & (col == 0), 1.0, 0.0)
    return jnp.where((row == 0) | (col == 0), grounded, full)


def eliminate(matrix, groups):
    n = matrix.shape[0]
    lane, top = iota((1, n), 1), iota((8, n), 0)

    def group(_, a):
        for s in range(8):
            pivot = 1.0 / a[s : s + 1, s : s + 1]
            hit = lane == s
            scaled = jnp.where(hit, pivot, a[s : s + 1, :] * pivot)
            a = jnp.where(hit, 0.0, a) - a[:, s : s + 1] * scaled
            a = jnp.concatenate([jnp.where(top == s, scaled, a[:8]), a[8:]], axis=0)
        a = jnp.concatenate([a[8:], a[:8]], axis=0)
        return pltpu.roll(a, n - 8, axis=1)

    return lax.fori_loop(0, groups, group, matrix)


def ungrounded(inverse):
    row, col = iota(inverse.shape, 0), iota(inverse.shape, 1)
    return jnp.where((row == 0) | (col == 0), 0.0, inverse)


def box_weights():
    source, out = iota((COLS, COLS), 0), iota((COLS, COLS), 1)
    own = (source >= out - HALO) & (source < out + HALO)
    side = jnp.where(source >= 4 * HALO, source - 4 * HALO, source)
    for step in (2, 1):
        side = jnp.where(side >= step * HALO, side - step * HALO, side)
    left = (source < 4 * HALO) & (out <= side)
    right = (source >= 4 * HALO) & (source < 8 * HALO) & (out >= side + COLS - HALO + 1)
    return jnp.concatenate(
        [jnp.where(own, 1.0, 0.0), jnp.where(left | right, 1.0, 0.0)], axis=0
    ).astype(BF16)


def kernel(
    n_acq, n_col,
    x_hbm, live_hbm, disp_ref, res_ref,
    main, edges, packed, lhs_hi, lhs_lo, weights, ypad, scale, obs, obs_in, rhs, disp,
    inverse, p2_chip, p2_recv, sol, p3_recv,
    x_ref, live_ref, live_smem, own_sem, live_sem, main_send, main_recv, edge_send, edge_recv,
    obs_ss, obs_rs, p2_ss, p2_rs, p3_ss, p3_rs, fw_ss, fw_rs,
):
    me, col = lax.axis_index("acq"), lax.axis_index("col")
    left, right = rem(col - 1, n_col), rem(col + 1, n_col)
    core, chip = lax.rem(me, 2), me // 2
    chips = n_acq // 2
    sibling = me + 1 - 2 * core
    lane = iota((ROWS, COLS), 1)

    fetch = pltpu.make_async_copy(x_hbm, x_ref, own_sem)
    fetch.start()
    lives = [
        pltpu.make_async_copy(live_hbm, live_ref, live_sem.at[0]),
        pltpu.make_async_copy(live_hbm, live_smem, live_sem.at[1]),
    ]
    for copy in lives:
        copy.start()

    barrier = pltpu.get_barrier_semaphore()

    def greet(target, where):
        pl.semaphore_signal(barrier, inc=1, device_id=(target, where), device_id_type=MESH)

    greet(sibling, col)

    @pl.loop(1, chips, unroll=True)
    def _(i):
        greet(2 * rem(chip + i, chips) + core, col)

    for i in (-2, -1, 1, 2):
        greet(2 * rem(chip + i, chips) + 1 - core, col)
    for side in (left, right):

        @pl.loop(-2, 3, unroll=True)
        def _(i):
            greet(2 * rem(chip + i, chips), side)
            greet(2 * rem(chip + i, chips) + 1, side)

    fetch.wait()
    to_right = jnp.zeros((ROWS, COLS), F32)
    to_left = jnp.zeros((ROWS, COLS), F32)
    for m in range(2):
        for i in range(LOCAL):
            base = 4 * HALO * m + HALO * i
            hit = (lane >= base) & (lane < base + HALO)
            value = x_ref[i, m]
            to_right = jnp.where(hit, pltpu.roll(value, (base + HALO) % COLS, axis=1), to_right)
            to_left = jnp.where(hit, pltpu.roll(value, base, axis=1) if base else value, to_left)
    packed[0] = to_right
    packed[1] = to_left

    pl.semaphore_wait(barrier, chips + 4 + 20)

    def window(of_core):
        return pl.ds(pl.multiple_of(8 * of_core, 8), PART)

    def block(index):
        return main.at[pl.ds(LOCAL * index, LOCAL)]

    own = pltpu.make_async_copy(x_ref.at[:, :, window(core)], block(core), main_recv.at[core])
    own.start()
    sends, late_sends = [], []

    def send_block(number, target, of_core, index):
        return pltpu.make_async_remote_copy(
            x_ref.at[:, :, window(of_core)], block(index), main_send.at[number], main_recv.at[index],
            device_id=(target, col), device_id_type=MESH,
        )

    def send_edge(number, target, of_core, index, side):
        return pltpu.make_async_remote_copy(
            packed.at[side, window(of_core)], edges.at[index, side],
            edge_send.at[number, side], edge_recv.at[index, side],
            device_id=(target, (right, left)[side]), device_id_type=MESH,
        )

    for side in range(2):
        for to in range(2):
            sends.append(send_edge(to, 2 * chip + to, to, core, side))
    sends.append(send_block(0, sibling, 1 - core, core))
    earlier = 2 * rem(chip - 1, chips)
    for to in range(2):
        sends.append(send_block(1 + to, earlier + to, to, 2 + core))
    for to in range(2):
        for side in range(2):
            sends.append(send_edge(2 + to, earlier + to, to, 2 + core, side))
    earlier = 2 * rem(chip - 2, chips)
    for to in range(2):
        late_sends.append(send_block(3 + to, earlier + to, to, 4))
        for side in range(2):
            late_sends.append(send_edge(4 + to, earlier + to, to, 4, side))
    for copy in sends:
        copy.start()

    @pl.when(core == 0)
    def _():
        for copy in late_sends:
            copy.start()

    for copy in lives:
        copy.wait()
    inverse[...] = eliminate(normal_matrix(live_ref[...]), FIRST_GROUPS)
    weights[...] = box_weights()
    ypad[...] = jnp.zeros(ypad.shape, F32)
    rhs[...] = jnp.zeros(rhs.shape, F32)

    keep_left = jnp.where(col > 0, 1.0, 0.0)
    keep_right = jnp.where(col < n_col - 1, 1.0, 0.0)
    lane = iota((PART, COLS), 1)
    in_left = lane < 4 * HALO
    in_right = (lane >= 4 * HALO) & (lane < 8 * HALO)

    def slot_of(lanes, i):
        place = jnp.where(lanes >= 4 * HALO, lanes - 4 * HALO, lanes)
        return (place >= HALO * i) & (place < HALO * (i + 1)) & (lanes < 8 * HALO)

    lane_wide = iota((GROUP, COLS), 1)
    slots = [jnp.where(slot_of(lane_wide, i), 1.0, 0.0).astype(BF16) for i in range(LOCAL)]

    def turned(value, by):
        return pltpu.roll(value, by % COLS, axis=1) if by % COLS else value

    at_row = 0
    own_real, own_imag = [], []
    for b in range(5):
        pltpu.make_async_copy(block(b), block(b), main_recv.at[b]).wait()
        for side in range(2):
            pltpu.make_async_copy(edges.at[b, side], edges.at[b, side], edge_recv.at[b, side]).wait()
        low, high = edges[b, 0] * keep_left, edges[b, 1] * keep_right
        real = jnp.where(in_left, low, jnp.where(in_right, turned(high, 4 * HALO), 0.0))
        imag = jnp.where(in_left, turned(low, -4 * HALO), jnp.where(in_right, high, 0.0))
        if b < 2:
            own_real.append(real)
            own_imag.append(imag)
        first_row = at_row
        edge_power = real * real + imag * imag
        for h in range(2):
            parts, outer = [], []
            for i in (2 * h, 2 * h + 1):
                re, im = main[LOCAL * b + i, 0], main[LOCAL * b + i, 1]
                parts.append(re * re + im * im)
                outer.append(jnp.where(slot_of(lane, i), edge_power, 0.0))
            at = pl.ds(at_row, GROUP)
            lhs_hi[at, :COLS], lhs_lo[at, :COLS] = split(jnp.concatenate(parts, axis=0))
            lhs_hi[at, COLS:], lhs_lo[at, COLS:] = split(jnp.concatenate(outer, axis=0))
            at_row += GROUP
        pairs = []
        for q, t in [(q, t) for q in range(min(b + 1, 2)) for t in range(-3, 4)]:
            lag = 4 * (b - q) + t
            if not 1 <= lag <= LAGS:
                continue
            later_re, later_im = turned(real, -HALO * t), turned(imag, -HALO * t)
            side_hi, side_lo = split(
                jnp.concatenate(
                    [
                        own_real[q] * later_re + own_imag[q] * later_im,
                        own_imag[q] * later_re - own_real[q] * later_im,
                    ],
                    axis=0,
                )
            )
            for i in range(max(0, -t), min(LOCAL, LOCAL - t)):
                e = LOCAL * q + i
                re, im = main[e, 0], main[e, 1]
                re_j, im_j = main[e + lag, 0], main[e + lag, 1]
                cross = jnp.concatenate([re * re_j + im * im_j, im * re_j - re * im_j], axis=0)
                at = pl.ds(at_row, GROUP)
                lhs_hi[at, :COLS], lhs_lo[at, :COLS] = split(cross)
                lhs_hi[at, COLS:] = side_hi * slots[i]
                lhs_lo[at, COLS:] = side_lo * slots[i]
                at_row += GROUP
                pairs.append((e, lag))

        at = pl.ds(first_row, at_row - first_row)
        by_cols = jnp.dot(lhs_hi[at, :], weights[...], preferred_element_type=F32)
        by_cols = by_cols + jnp.dot(lhs_lo[at, :], weights[...], preferred_element_type=F32)
        first, count = first_row // PART, (at_row - first_row) // PART
        ypad[pl.ds(first, count), 8 : 8 + PART, :] = by_cols.reshape(count, PART, COLS)

        def looked(i):
            total = ypad[i, 6 : 6 + PART, :]
            for step in range(1, 5):
                total = total + ypad[i, 6 + step : 6 + step + PART, :]
            return total

        for i in range(LOCAL):
            scale[LOCAL * b + i] = lax.rsqrt(looked(first + i))
        for place, (e, lag) in enumerate(pairs):
            live = jnp.where(live_smem[lag - 1, PAIR * chip + e] > 0, 1.0, 0.0)
            factor = scale[e] * scale[e + lag] * live
            for m in range(2):
                value = looked(first + LOCAL + 2 * place + m) * factor
                obs[e // LOCAL, e % LOCAL, lag - 1, m] = value
                rhs[m, e] = rhs[m, e] - value
                rhs[m, e + lag] = rhs[m, e + lag] + value

    for m in range(2):
        for j in range(CHAIN):
            p2_chip[pl.ds(8 * (j // 4) + 4 * m + j % 4, PART, stride=WIDE), :] = rhs[m, j]

    z, x = chip // 2, lax.rem(chip, 2)
    planes = n_acq // 4
    half = HALF
    skip = 4 * core

    def place(zt, xt):
        both = lax.rem(zt, 2) == core
        return both | (xt == lax.rem(zt // 2 + core, 2)), 3 * (zt // 2) + jnp.where(both, xt, 2)

    def plane(turn):
        away = (planes - turn) // 2
        return rem(jnp.where(lax.rem(turn, 2) == 1, z + away, z - away), planes)

    is_owner, row_me = place(z, x)

    @pl.loop(0, planes, unroll=True)
    def _(turn):
        zt = plane(turn)
        for xt in range(2):
            owns, u = place(zt, xt)
            target = 4 * zt + 2 * xt + core

            @pl.when(owns & (target != me))
            def _():
                pltpu.make_async_remote_copy(
                    p2_chip.at[pl.ds(pl.multiple_of((u + skip) * WIDE, 8), WIDE)],
                    p2_recv.at[pl.ds(pl.multiple_of(chip * WIDE, 8), WIDE)],
                    p2_ss, p2_rs, device_id=(target, col), device_id_type=MESH,
                ).start()

    to_sibling = pltpu.make_async_remote_copy(
        obs.at[1 - core], obs_in, obs_ss, obs_rs, device_id=(sibling, col), device_id_type=MESH
    )
    to_sibling.start()

    def wait(ref, blocks, sem):
        part = ref.at[pl.ds(0, blocks * WIDE)]
        pltpu.make_async_copy(part, part, sem).wait()

    row_at = pl.multiple_of((core * half + row_me) * WIDE, 8)

    @pl.when(is_owner)
    def _():
        inverse[...] = ungrounded(eliminate(inverse[...], 16 - FIRST_GROUPS))
        p2_recv[pl.ds(pl.multiple_of(chip * WIDE, 8), WIDE), :] = p2_chip[
            pl.ds(pl.multiple_of((row_me + skip) * WIDE, 8), WIDE), :
        ]
        wait(p2_recv, chips - 1, p2_rs)
        groups = []
        for b in range(n_acq):
            total = None
            for g in range(b % 2, 5, 2):
                c = (b - g) // 2
                if c >= 0:
                    part = p2_recv[c * WIDE + 8 * g : c * WIDE + 8 * g + 8, :]
                    total = part if total is None else total + part
            groups.append(total)
        low = iota((8, COLS), 0) < 4
        first, second = [], []
        for v in range(n_acq // 2):
            one, two = groups[2 * v], groups[2 * v + 1]
            first.append(jnp.where(low, one, pltpu.roll(two, 4, axis=0)))
            second.append(jnp.where(low, pltpu.roll(one, 4, axis=0), two))
        sums = jnp.concatenate(
            [jnp.concatenate(first, axis=0), jnp.concatenate(second, axis=0)], axis=1
        )
        solved = jnp.dot(
            inverse[...], sums, precision=lax.Precision.HIGHEST, preferred_element_type=F32
        )
        for v in range(n_acq // 2):
            one, two = solved[8 * v : 8 * v + 8, :COLS], solved[8 * v : 8 * v + 8, COLS:]
            sol[16 * v : 16 * v + 8, :] = jnp.where(low, one, pltpu.roll(two, 4, axis=0))
            sol[16 * v + 8 : 16 * v + 16, :] = jnp.where(low, pltpu.roll(one, 4, axis=0), two)
        sol[8 * n_acq :, :] = jnp.zeros((24, COLS), F32)

        @pl.loop(0, planes, unroll=True)
        def _(turn):
            zt = turn
            for xt in range(2):
                target = 4 * zt + 2 * xt + core

                @pl.when(target != me)
                def _():
                    pltpu.make_async_remote_copy(
                        sol.at[pl.ds(pl.multiple_of((2 * zt + xt) * 16, 8), WIDE)],
                        p3_recv.at[pl.ds(row_at, WIDE)],
                        p3_ss, p3_rs, device_id=(target, col), device_id_type=MESH,
                    ).start()

        p3_recv[pl.ds(row_at, WIDE), :] = sol[pl.ds(pl.multiple_of(chip * 16, 8), WIDE), :]

    to_sibling.wait()
    upper = iota((8, COLS), 0) < 4
    on_first = core == 0

    @pl.loop(0, LAGS)
    def _(k):
        for e in range(LOCAL):
            for m in range(2):
                mine, other = obs[core, e, k, m], obs_in[e, k, m]
                low, high = jnp.where(on_first, mine, other), jnp.where(on_first, other, mine)
                res_ref[e, k, m] = jnp.concatenate(
                    [low[:8], jnp.where(upper, low[8:], high[:8]), high[8:]], axis=0
                )

    @pl.when(is_owner)
    def _():
        wait(p3_recv, half - 1, p3_rs)

    @pl.when(jnp.logical_not(is_owner))
    def _():
        wait(p3_recv, half, p3_rs)

    own_half = pl.ds(pl.multiple_of(core * half * WIDE, 8), half * WIDE)
    forward = pltpu.make_async_remote_copy(
        p3_recv.at[own_half], p3_recv.at[own_half], fw_ss, fw_rs,
        device_id=(sibling, col), device_id_type=MESH,
    )
    forward.start()
    forward.wait()

    for m in range(2):
        for j in range(16):
            disp[m, j] = p3_recv[pl.ds(8 * core + 8 * (j // 4) + 4 * m + j % 4, ROWS, stride=WIDE), :]
    for e in range(LOCAL):
        for m in range(2):
            disp_ref[e, m] = disp[m, e]

    @pl.loop(0, LAGS, unroll=3)
    def _(k):
        for e in range(LOCAL):
            live = jnp.where(live_smem[k, LOCAL * me + e] > 0, 1.0, 0.0)
            for m in range(2):
                res_ref[e, k, m] = res_ref[e, k, m] - (disp[m, e + k + 1] - disp[m, e]) * live

    @pl.when(is_owner)
    def _():
        wait(p2_chip, half - 1, p2_ss)
        wait(p2_recv, chips - 1, p3_ss)

    @pl.when(jnp.logical_not(is_owner))
    def _():
        wait(p2_chip, half, p2_ss)

    for copy in sends:
        copy.wait_send()

    @pl.when(core == 0)
    def _():
        for copy in late_sends:
            copy.wait_send()


def place_out(disp_in, res_in, disp_out, res_out, sems):
    copies = [pltpu.make_async_copy(disp_in, disp_out, sems.at[LOCAL])]
    for e in range(LOCAL):
        copies.append(pltpu.make_async_copy(res_in.at[e], res_out.at[e], sems.at[e]))
    for copy in copies:
        copy.start()
    for copy in copies:
        copy.wait()


def per_device(n_acq, n_col, samples, pair_live):
    vmem = pltpu.VMEM
    rows_all = CHAIN * PART + LAGS * PAIR * GROUP
    results = pl.pallas_call(
        functools.partial(kernel, n_acq, n_col),
        out_shape=(
            jax.ShapeDtypeStruct((LOCAL, 2, ROWS, COLS), F32),
            jax.ShapeDtypeStruct((LOCAL, LAGS, 2, ROWS, COLS), F32),
        ),
        in_specs=[
            pl.BlockSpec(memory_space=pltpu.HBM),
            pl.BlockSpec(memory_space=pltpu.HBM),
        ],
        out_specs=(pl.BlockSpec(memory_space=pltpu.VMEM), pl.BlockSpec(memory_space=pltpu.VMEM)),
        scratch_shapes=[
            vmem((CHAIN, 2, PART, COLS), F32),
            vmem((5, 2, PART, COLS), F32),
            vmem((2, ROWS, COLS), F32),
            vmem((rows_all, 2 * COLS), BF16),
            vmem((rows_all, 2 * COLS), BF16),
            vmem((2 * COLS, COLS), BF16),
            vmem((rows_all // PART, 32, COLS), F32),
            vmem((CHAIN, PART, COLS), F32),
            vmem((2, LOCAL, LAGS, 2, PART, COLS), F32),
            vmem((LOCAL, LAGS, 2, PART, COLS), F32),
            vmem((2, CHAIN, PART, COLS), F32),
            vmem((2, 16, ROWS, COLS), F32),
            vmem((128, 128), F32),
            vmem((PART * WIDE, COLS), F32),
            vmem((n_acq // 2 * WIDE, COLS), F32),
            vmem((8 * n_acq + 24, COLS), F32),
            vmem((ROWS * WIDE, COLS), F32),
            vmem((LOCAL, 2, ROWS, COLS), F32),
            vmem((LAGS, 4 * n_acq), jnp.int32),
            pltpu.SMEM((LAGS, 4 * n_acq), jnp.int32),
            pltpu.SemaphoreType.DMA,
            pltpu.SemaphoreType.DMA((2,)),
            pltpu.SemaphoreType.DMA((5,)),
            pltpu.SemaphoreType.DMA((5,)),
            pltpu.SemaphoreType.DMA((6, 2)),
            pltpu.SemaphoreType.DMA((5, 2)),
        ] + [pltpu.SemaphoreType.DMA] * 8,
        compiler_params=pltpu.CompilerParams(
            collective_id=0, has_side_effects=True, vmem_limit_bytes=32 * 1024 * 1024
        ),
    )(pltpu.with_memory_space_constraint(samples, pltpu.HBM), pltpu.with_memory_space_constraint(pair_live.T, pltpu.HBM))
    return pl.pallas_call(
        place_out,
        out_shape=tuple(jax.ShapeDtypeStruct(r.shape, F32) for r in results),
        in_specs=[pl.BlockSpec(memory_space=pl.ANY)] * 2,
        out_specs=(pl.BlockSpec(memory_space=pl.ANY),) * 2,
        scratch_shapes=[pltpu.SemaphoreType.DMA((LOCAL + 1,))],
        compiler_params=pltpu.CompilerParams(vmem_limit_bytes=4 * 1024 * 1024),
    )(*results)


def solution(mesh):
    return jax.shard_map(
        functools.partial(per_device, mesh.shape["acq"], mesh.shape["col"]),
        mesh=mesh,
        in_specs=(P("acq", None, None, "col"), P()),
        out_specs=(P("acq", None, None, "col"), P("acq", None, None, None, "col")),
        check_vma=False,
    )
```

```python
import functools

import jax
import jax.numpy as jnp
from jax import lax
from jax.experimental import pallas as pl
from jax.experimental.pallas import tpu as pltpu
from jax.sharding import PartitionSpec as P

MESH = pl.DeviceIdType.MESH
F32 = jnp.float32
BF16 = jnp.bfloat16
LOCAL = 4
PAIR = 8
CHAIN = 20
LAGS = 12
ROWS = 24
HALF = 12
PART = 16
COLS = 128
GROUP = 32
HALO = 10
WIDE = 40
FIRST_GROUPS = 5


def rem(a, n):
    return lax.rem(a + 4 * n, n)


def iota(shape, dim):
    return lax.broadcasted_iota(jnp.int32, shape, dim)


def split(value):
    high = value.astype(BF16)
    return high, (value - high.astype(F32)).astype(BF16)


def normal_matrix(live):
    n = live.shape[1]
    row, col = iota((n, n), 0), iota((n, n), 1)
    lower = jnp.zeros((n, n), F32)
    for k in range(LAGS):
        weight = jnp.where(live[k : k + 1, :] > 0, 1.0, 0.0)
        lower = lower + jnp.where(row == col + (k + 1), weight, 0.0)
    both = lower + lower.T
    degree = jnp.sum(both, axis=1, keepdims=True)
    full = jnp.where(row == col, degree, -both)
    grounded = jnp.where((row == 0) & (col == 0), 1.0, 0.0)
    return jnp.where((row == 0) | (col == 0), grounded, full)


def eliminate(matrix, groups):
    n = matrix.shape[0]
    lane, top = iota((1, n), 1), iota((8, n), 0)

    def group(_, a):
        for s in range(8):
            pivot = 1.0 / a[s : s + 1, s : s + 1]
            hit = lane == s
            scaled = jnp.where(hit, pivot, a[s : s + 1, :] * pivot)
            a = jnp.where(hit, 0.0, a) - a[:, s : s + 1] * scaled
            a = jnp.concatenate([jnp.where(top == s, scaled, a[:8]), a[8:]], axis=0)
        a = jnp.concatenate([a[8:], a[:8]], axis=0)
        return pltpu.roll(a, n - 8, axis=1)

    return lax.fori_loop(0, groups, group, matrix)


def ungrounded(inverse):
    row, col = iota(inverse.shape, 0), iota(inverse.shape, 1)
    return jnp.where((row == 0) | (col == 0), 0.0, inverse)


def box_weights():
    source, out = iota((COLS, COLS), 0), iota((COLS, COLS), 1)
    own = (source >= out - HALO) & (source < out + HALO)
    side = jnp.where(source >= 4 * HALO, source - 4 * HALO, source)
    for step in (2, 1):
        side = jnp.where(side >= step * HALO, side - step * HALO, side)
    left = (source < 4 * HALO) & (out <= side)
    right = (source >= 4 * HALO) & (source < 8 * HALO) & (out >= side + COLS - HALO + 1)
    return jnp.concatenate(
        [jnp.where(own, 1.0, 0.0), jnp.where(left | right, 1.0, 0.0)], axis=0
    ).astype(BF16)


def kernel(
    n_acq, n_col,
    x_hbm, live_hbm, disp, res_ref, flags,
    main, edges, packed, lhs_hi, lhs_lo, weights, ypad, scale, obs, obs_in, rhs,
    inverse, p2_chip, p2_recv, sol, p3_recv,
    x_ref, live_ref, live_smem, own_sem, live_sem, main_send, main_recv, edge_send, edge_recv,
    obs_ss, obs_rs, p2_ss, p2_rs, p3_ss, p3_rs, fw_ss, fw_rs,
):
    me, col = lax.axis_index("acq"), lax.axis_index("col")
    left, right = rem(col - 1, n_col), rem(col + 1, n_col)
    core, chip = lax.rem(me, 2), me // 2
    chips = n_acq // 2
    sibling = me + 1 - 2 * core
    lane = iota((ROWS, COLS), 1)

    fetch = pltpu.make_async_copy(x_hbm, x_ref, own_sem)
    fetch.start()
    lives = [
        pltpu.make_async_copy(live_hbm, live_ref, live_sem.at[0]),
        pltpu.make_async_copy(live_hbm, live_smem, live_sem.at[1]),
    ]
    for copy in lives:
        copy.start()

    barrier = pltpu.get_barrier_semaphore()

    def greet(target, where):
        pl.semaphore_signal(barrier, inc=1, device_id=(target, where), device_id_type=MESH)

    greet(sibling, col)

    @pl.loop(1, chips, unroll=True)
    def _(i):
        greet(2 * rem(chip + i, chips) + core, col)

    for i in (-2, -1, 1, 2):
        greet(2 * rem(chip + i, chips) + 1 - core, col)
    for side in (left, right):

        @pl.loop(-2, 3, unroll=True)
        def _(i):
            greet(2 * rem(chip + i, chips), side)
            greet(2 * rem(chip + i, chips) + 1, side)

    fetch.wait()
    to_right = jnp.zeros((ROWS, COLS), F32)
    to_left = jnp.zeros((ROWS, COLS), F32)
    for m in range(2):
        for i in range(LOCAL):
            base = 4 * HALO * m + HALO * i
            hit = (lane >= base) & (lane < base + HALO)
            value = x_ref[i, m]
            to_right = jnp.where(hit, pltpu.roll(value, (base + HALO) % COLS, axis=1), to_right)
            to_left = jnp.where(hit, pltpu.roll(value, base, axis=1) if base else value, to_left)
    packed[0] = to_right
    packed[1] = to_left

    pl.semaphore_wait(barrier, chips + 4 + 20)

    def window(of_core):
        return pl.ds(pl.multiple_of(8 * of_core, 8), PART)

    def block(index):
        return main.at[pl.ds(LOCAL * index, LOCAL)]

    own = pltpu.make_async_copy(x_ref.at[:, :, window(core)], block(core), main_recv.at[core])
    own.start()
    sends, late_sends = [], []

    def send_block(number, target, of_core, index):
        return pltpu.make_async_remote_copy(
            x_ref.at[:, :, window(of_core)], block(index), main_send.at[number], main_recv.at[index],
            device_id=(target, col), device_id_type=MESH,
        )

    def send_edge(number, target, of_core, index, side):
        return pltpu.make_async_remote_copy(
            packed.at[side, window(of_core)], edges.at[index, side],
            edge_send.at[number, side], edge_recv.at[index, side],
            device_id=(target, (right, left)[side]), device_id_type=MESH,
        )

    for side in range(2):
        for to in range(2):
            sends.append(send_edge(to, 2 * chip + to, to, core, side))
    sends.append(send_block(0, sibling, 1 - core, core))
    earlier = 2 * rem(chip - 1, chips)
    for to in range(2):
        sends.append(send_block(1 + to, earlier + to, to, 2 + core))
    for to in range(2):
        for side in range(2):
            sends.append(send_edge(2 + to, earlier + to, to, 2 + core, side))
    earlier = 2 * rem(chip - 2, chips)
    for to in range(2):
        late_sends.append(send_block(3 + to, earlier + to, to, 4))
        for side in range(2):
            late_sends.append(send_edge(4 + to, earlier + to, to, 4, side))
    for copy in sends:
        copy.start()

    @pl.when(core == 0)
    def _():
        for copy in late_sends:
            copy.start()

    for copy in lives:
        copy.wait()
    inverse[...] = eliminate(normal_matrix(live_ref[...]), FIRST_GROUPS)
    weights[...] = box_weights()
    ypad[...] = jnp.zeros(ypad.shape, F32)
    rhs[...] = jnp.zeros(rhs.shape, F32)

    keep_left = jnp.where(col > 0, 1.0, 0.0)
    keep_right = jnp.where(col < n_col - 1, 1.0, 0.0)
    lane = iota((PART, COLS), 1)
    in_left = lane < 4 * HALO
    in_right = (lane >= 4 * HALO) & (lane < 8 * HALO)

    def slot_of(lanes, i):
        place = jnp.where(lanes >= 4 * HALO, lanes - 4 * HALO, lanes)
        return (place >= HALO * i) & (place < HALO * (i + 1)) & (lanes < 8 * HALO)

    lane_wide = iota((GROUP, COLS), 1)
    slots = [jnp.where(slot_of(lane_wide, i), 1.0, 0.0).astype(BF16) for i in range(LOCAL)]

    def turned(value, by):
        return pltpu.roll(value, by % COLS, axis=1) if by % COLS else value

    at_row = 0
    own_real, own_imag = [], []
    for b in range(5):
        pltpu.make_async_copy(block(b), block(b), main_recv.at[b]).wait()
        for side in range(2):
            pltpu.make_async_copy(edges.at[b, side], edges.at[b, side], edge_recv.at[b, side]).wait()
        low, high = edges[b, 0] * keep_left, edges[b, 1] * keep_right
        real = jnp.where(in_left, low, jnp.where(in_right, turned(high, 4 * HALO), 0.0))
        imag = jnp.where(in_left, turned(low, -4 * HALO), jnp.where(in_right, high, 0.0))
        if b < 2:
            own_real.append(real)
            own_imag.append(imag)
        first_row = at_row
        edge_power = real * real + imag * imag
        for h in range(2):
            parts, outer = [], []
            for i in (2 * h, 2 * h + 1):
                re, im = main[LOCAL * b + i, 0], main[LOCAL * b + i, 1]
                parts.append(re * re + im * im)
                outer.append(jnp.where(slot_of(lane, i), edge_power, 0.0))
            at = pl.ds(at_row, GROUP)
            lhs_hi[at, :COLS], lhs_lo[at, :COLS] = split(jnp.concatenate(parts, axis=0))
            lhs_hi[at, COLS:], lhs_lo[at, COLS:] = split(jnp.concatenate(outer, axis=0))
            at_row += GROUP
        pairs = []
        for q, t in [(q, t) for q in range(min(b + 1, 2)) for t in range(-3, 4)]:
            lag = 4 * (b - q) + t
            if not 1 <= lag <= LAGS:
                continue
            later_re, later_im = turned(real, -HALO * t), turned(imag, -HALO * t)
            side_hi, side_lo = split(
                jnp.concatenate(
                    [
                        own_real[q] * later_re + own_imag[q] * later_im,
                        own_imag[q] * later_re - own_real[q] * later_im,
                    ],
                    axis=0,
                )
            )
            for i in range(max(0, -t), min(LOCAL, LOCAL - t)):
                e = LOCAL * q + i
                re, im = main[e, 0], main[e, 1]
                re_j, im_j = main[e + lag, 0], main[e + lag, 1]
                cross = jnp.concatenate([re * re_j + im * im_j, im * re_j - re * im_j], axis=0)
                at = pl.ds(at_row, GROUP)
                lhs_hi[at, :COLS], lhs_lo[at, :COLS] = split(cross)
                lhs_hi[at, COLS:] = side_hi * slots[i]
                lhs_lo[at, COLS:] = side_lo * slots[i]
                at_row += GROUP
                pairs.append((e, lag))

        at = pl.ds(first_row, at_row - first_row)
        by_cols = jnp.dot(lhs_hi[at, :], weights[...], preferred_element_type=F32)
        by_cols = by_cols + jnp.dot(lhs_lo[at, :], weights[...], preferred_element_type=F32)
        first, count = first_row // PART, (at_row - first_row) // PART
        ypad[pl.ds(first, count), 8 : 8 + PART, :] = by_cols.reshape(count, PART, COLS)

        def looked(i):
            total = ypad[i, 6 : 6 + PART, :]
            for step in range(1, 5):
                total = total + ypad[i, 6 + step : 6 + step + PART, :]
            return total

        for i in range(LOCAL):
            scale[LOCAL * b + i] = lax.rsqrt(looked(first + i))
        for place, (e, lag) in enumerate(pairs):
            live = jnp.where(live_smem[lag - 1, PAIR * chip + e] > 0, 1.0, 0.0)
            factor = scale[e] * scale[e + lag] * live
            for m in range(2):
                value = looked(first + LOCAL + 2 * place + m) * factor
                obs[e // LOCAL, e % LOCAL, lag - 1, m] = value
                rhs[m, e] = rhs[m, e] - value
                rhs[m, e + lag] = rhs[m, e + lag] + value

    for m in range(2):
        for j in range(CHAIN):
            p2_chip[pl.ds(8 * (j // 4) + 4 * m + j % 4, PART, stride=WIDE), :] = rhs[m, j]

    z, x = chip // 2, lax.rem(chip, 2)
    planes = n_acq // 4
    half = HALF
    skip = 4 * core

    def place(zt, xt):
        both = lax.rem(zt, 2) == core
        return both | (xt == lax.rem(zt // 2 + core, 2)), 3 * (zt // 2) + jnp.where(both, xt, 2)

    def plane(turn):
        away = (planes - turn) // 2
        return rem(jnp.where(lax.rem(turn, 2) == 1, z + away, z - away), planes)

    is_owner, row_me = place(z, x)

    @pl.loop(0, planes, unroll=True)
    def _(turn):
        zt = plane(turn)
        for xt in range(2):
            owns, u = place(zt, xt)
            target = 4 * zt + 2 * xt + core

            @pl.when(owns & (target != me))
            def _():
                pltpu.make_async_remote_copy(
                    p2_chip.at[pl.ds(pl.multiple_of((u + skip) * WIDE, 8), WIDE)],
                    p2_recv.at[pl.ds(pl.multiple_of(chip * WIDE, 8), WIDE)],
                    p2_ss, p2_rs, device_id=(target, col), device_id_type=MESH,
                ).start()

    to_sibling = pltpu.make_async_remote_copy(
        obs.at[1 - core], obs_in, obs_ss, obs_rs, device_id=(sibling, col), device_id_type=MESH
    )
    to_sibling.start()

    def wait(ref, blocks, sem):
        part = ref.at[pl.ds(0, blocks * WIDE)]
        pltpu.make_async_copy(part, part, sem).wait()

    row_at = pl.multiple_of((core * half + row_me) * WIDE, 8)

    @pl.when(is_owner)
    def _():
        inverse[...] = ungrounded(eliminate(inverse[...], 16 - FIRST_GROUPS))
        p2_recv[pl.ds(pl.multiple_of(chip * WIDE, 8), WIDE), :] = p2_chip[
            pl.ds(pl.multiple_of((row_me + skip) * WIDE, 8), WIDE), :
        ]
        wait(p2_recv, chips - 1, p2_rs)
        groups = []
        for b in range(n_acq):
            total = None
            for g in range(b % 2, 5, 2):
                c = (b - g) // 2
                if c >= 0:
                    part = p2_recv[c * WIDE + 8 * g : c * WIDE + 8 * g + 8, :]
                    total = part if total is None else total + part
            groups.append(total)
        low = iota((8, COLS), 0) < 4
        first, second = [], []
        for v in range(n_acq // 2):
            one, two = groups[2 * v], groups[2 * v + 1]
            first.append(jnp.where(low, one, pltpu.roll(two, 4, axis=0)))
            second.append(jnp.where(low, pltpu.roll(one, 4, axis=0), two))
        sums = jnp.concatenate(
            [jnp.concatenate(first, axis=0), jnp.concatenate(second, axis=0)], axis=1
        )
        solved = jnp.dot(
            inverse[...], sums, precision=lax.Precision.HIGHEST, preferred_element_type=F32
        )
        for v in range(n_acq // 2):
            one, two = solved[8 * v : 8 * v + 8, :COLS], solved[8 * v : 8 * v + 8, COLS:]
            sol[16 * v : 16 * v + 8, :] = jnp.where(low, one, pltpu.roll(two, 4, axis=0))
            sol[16 * v + 8 : 16 * v + 16, :] = jnp.where(low, pltpu.roll(one, 4, axis=0), two)
        sol[8 * n_acq :, :] = jnp.zeros((24, COLS), F32)

        @pl.loop(0, planes, unroll=True)
        def _(turn):
            zt = turn
            for xt in range(2):
                target = 4 * zt + 2 * xt + core

                @pl.when(target != me)
                def _():
                    pltpu.make_async_remote_copy(
                        sol.at[pl.ds(pl.multiple_of((2 * zt + xt) * 16, 8), WIDE)],
                        p3_recv.at[pl.ds(row_at, WIDE)],
                        p3_ss, p3_rs, device_id=(target, col), device_id_type=MESH,
                    ).start()

        p3_recv[pl.ds(row_at, WIDE), :] = sol[pl.ds(pl.multiple_of(chip * 16, 8), WIDE), :]

    to_sibling.wait()
    upper = iota((8, COLS), 0) < 4
    on_first = core == 0

    @pl.loop(0, LAGS)
    def _(k):
        for e in range(LOCAL):
            live = jnp.where(live_smem[k, LOCAL * me + e] > 0, 1.0, 0.0)
            flags[LOCAL * k + e] = jnp.full((8, COLS), live, F32)
            for m in range(2):
                mine, other = obs[core, e, k, m], obs_in[e, k, m]
                low, high = jnp.where(on_first, mine, other), jnp.where(on_first, other, mine)
                res_ref[e, k, m] = jnp.concatenate(
                    [low[:8], jnp.where(upper, low[8:], high[:8]), high[8:]], axis=0
                )

    @pl.when(is_owner)
    def _():
        wait(p3_recv, half - 1, p3_rs)

    @pl.when(jnp.logical_not(is_owner))
    def _():
        wait(p3_recv, half, p3_rs)

    own_half = pl.ds(pl.multiple_of(core * half * WIDE, 8), half * WIDE)
    forward = pltpu.make_async_remote_copy(
        p3_recv.at[own_half], p3_recv.at[own_half], fw_ss, fw_rs,
        device_id=(sibling, col), device_id_type=MESH,
    )
    forward.start()
    forward.wait()

    for m in range(2):
        for j in range(16):
            disp[m, j] = p3_recv[pl.ds(8 * core + 8 * (j // 4) + 4 * m + j % 4, ROWS, stride=WIDE), :]

    @pl.when(is_owner)
    def _():
        wait(p2_chip, half - 1, p2_ss)
        wait(p2_recv, chips - 1, p3_ss)

    @pl.when(jnp.logical_not(is_owner))
    def _():
        wait(p2_chip, half, p2_ss)

    for copy in sends:
        copy.wait_send()

    @pl.when(core == 0)
    def _():
        for copy in late_sends:
            copy.wait_send()


def finish(disp, seen, flags, disp_out, res_out, own, res, sems):
    for e in range(LOCAL):
        for m in range(2):
            own[e, m] = disp[m, e]
    copies = [pltpu.make_async_copy(own, disp_out, sems.at[LOCAL])]
    copies[0].start()
    for e in range(LOCAL):
        for k in range(LAGS):
            live = flags[LOCAL * k + e, 0:1, :]
            for m in range(2):
                res[e, k, m] = seen[e, k, m] - (disp[m, e + k + 1] - disp[m, e]) * live
        copies.append(pltpu.make_async_copy(res.at[e], res_out.at[e], sems.at[e]))
        copies[-1].start()
    for copy in copies:
        copy.wait()


def per_device(n_acq, n_col, samples, pair_live):
    vmem = pltpu.VMEM
    rows_all = CHAIN * PART + LAGS * PAIR * GROUP
    results = pl.pallas_call(
        functools.partial(kernel, n_acq, n_col),
        out_shape=(
            jax.ShapeDtypeStruct((2, 16, ROWS, COLS), F32),
            jax.ShapeDtypeStruct((LOCAL, LAGS, 2, ROWS, COLS), F32),
            jax.ShapeDtypeStruct((LOCAL * LAGS, 8, COLS), F32),
        ),
        in_specs=[
            pl.BlockSpec(memory_space=pltpu.HBM),
            pl.BlockSpec(memory_space=pltpu.HBM),
        ],
        out_specs=(pl.BlockSpec(memory_space=pltpu.VMEM),) * 3,
        scratch_shapes=[
            vmem((CHAIN, 2, PART, COLS), F32),
            vmem((5, 2, PART, COLS), F32),
            vmem((2, ROWS, COLS), F32),
            vmem((rows_all, 2 * COLS), BF16),
            vmem((rows_all, 2 * COLS), BF16),
            vmem((2 * COLS, COLS), BF16),
            vmem((rows_all // PART, 32, COLS), F32),
            vmem((CHAIN, PART, COLS), F32),
            vmem((2, LOCAL, LAGS, 2, PART, COLS), F32),
            vmem((LOCAL, LAGS, 2, PART, COLS), F32),
            vmem((2, CHAIN, PART, COLS), F32),
            vmem((128, 128), F32),
            vmem((PART * WIDE, COLS), F32),
            vmem((n_acq // 2 * WIDE, COLS), F32),
            vmem((8 * n_acq + 24, COLS), F32),
            vmem((ROWS * WIDE, COLS), F32),
            vmem((LOCAL, 2, ROWS, COLS), F32),
            vmem((LAGS, 4 * n_acq), jnp.int32),
            pltpu.SMEM((LAGS, 4 * n_acq), jnp.int32),
            pltpu.SemaphoreType.DMA,
            pltpu.SemaphoreType.DMA((2,)),
            pltpu.SemaphoreType.DMA((5,)),
            pltpu.SemaphoreType.DMA((5,)),
            pltpu.SemaphoreType.DMA((6, 2)),
            pltpu.SemaphoreType.DMA((5, 2)),
        ] + [pltpu.SemaphoreType.DMA] * 8,
        compiler_params=pltpu.CompilerParams(
            collective_id=0, has_side_effects=True, vmem_limit_bytes=32 * 1024 * 1024
        ),
    )(pltpu.with_memory_space_constraint(samples, pltpu.HBM), pltpu.with_memory_space_constraint(pair_live.T, pltpu.HBM))
    return pl.pallas_call(
        finish,
        out_shape=(
            jax.ShapeDtypeStruct((LOCAL, 2, ROWS, COLS), F32),
            jax.ShapeDtypeStruct((LOCAL, LAGS, 2, ROWS, COLS), F32),
        ),
        in_specs=[pl.BlockSpec(memory_space=pltpu.VMEM)] * 3,
        out_specs=(pl.BlockSpec(memory_space=pl.ANY),) * 2,
        scratch_shapes=[
            vmem((LOCAL, 2, ROWS, COLS), F32),
            vmem((LOCAL, LAGS, 2, ROWS, COLS), F32),
            pltpu.SemaphoreType.DMA((LOCAL + 1,)),
        ],
        compiler_params=pltpu.CompilerParams(vmem_limit_bytes=8 * 1024 * 1024),
    )(*results)


def solution(mesh):
    return jax.shard_map(
        functools.partial(per_device, mesh.shape["acq"], mesh.shape["col"]),
        mesh=mesh,
        in_specs=(P("acq", None, None, "col"), P()),
        out_specs=(P("acq", None, None, "col"), P("acq", None, None, None, "col")),
        check_vma=False,
    )
```
